768 devices in a mesh: tile: 128 (over z_hi, y, x, core), scene: 6 (over z_lo).
Axes of the slice: x: 4, y: 8, z: 12 (z_hi: 2, z_lo: 6; z = z_hi * 6 + z_lo), core: 2. Of those that a mesh axis runs over, the one named last changes fastest.
Arguments:
- features: bfloat16 [6, 384, 64, 128], P('scene', 'tile'), may hold values from -6 to 6
- cotangent: bfloat16 [6, 384, 64, 128], P('scene', 'tile'), may hold values from -6 to 6
- blocks: int32 [6, 384], P('scene', 'tile'), may hold values from 0 to 8, as said below
- w_first: bfloat16 [27, 128, 128], replicated, may hold values from -0.109375 to 0.109375
- w_second: bfloat16 [27, 128, 128], replicated, may hold values from -0.109375 to 0.109375
Outputs:
- block_out: bfloat16 [6, 384, 64, 128], P('scene', 'tile')
- input_grad: bfloat16 [6, 384, 64, 128], P('scene', 'tile')
- grad_first: float32 [27, 16384], P(None, 'tile')
- grad_second: float32 [27, 16384], P(None, 'tile')
The draws below stay inside these ranges and needn't reach their ends.
Inputs may be any that keep to these rules, and one draw needn't show every extreme that they name: In each tile's 3 slots the non-empty ones come first and name distinct blocks of 0 to 7; the rest hold 8. Every tile has at least 1 non-empty slot; in every scene some tile has all 3 slots non-empty and some other tile the fewest.
All inputs are finite; a program needn't handle non-finite values.
Results may differ from the reference program's by a relative error of at most 0.0029.
Values may be sent and summed in bfloat16 or wider, within the bound.
No kernel may reach another device: no remote copies, remote signals or barrier semaphores. Data moves between devices by JAX's collectives and lax.ppermute only.
A program may use at most 32 MiB of HBM per device.

```python
import jax
import jax.numpy as jnp
from jax import lax

C = 128
BY = 2
BZ = 4
CAP = 3
SCENES = 6
N_TILE = 128


def draw_blocks(key, part):
    key = jax.random.fold_in(key, 7)
    first_key, second_key, third_key = jax.random.split(key, 3)
    block_total = BY * BZ
    lowest = max(1, 3 * block_total // 20)
    device_total = SCENES * N_TILE
    counts = jax.random.randint(first_key, (device_total,), lowest, CAP + 1)
    chosen = jax.random.randint(second_key, (SCENES,), 0, N_TILE)
    positions = jnp.arange(device_total)
    scene_place = positions // N_TILE
    tile_place = positions % N_TILE
    counts = jnp.where(tile_place == chosen[scene_place], CAP, counts)
    counts = jnp.where(tile_place == (chosen[scene_place] + 1) % N_TILE, lowest, counts)
    orders = jax.vmap(lambda sub_key: jax.random.permutation(sub_key, block_total))(jax.random.split(third_key, device_total))
    slot_range = jnp.arange(CAP)
    picked = jnp.where(slot_range[None, :] < counts[:, None], orders[:, :CAP], block_total)
    return picked.reshape(SCENES, N_TILE * CAP).astype(jnp.int32)


def block_levels(stream_key, extent, pieces, least, largest):
    loudness = 1.0
    for axis_at, shards_of in pieces:
        heights = jax.random.uniform(jax.random.fold_in(jax.random.fold_in(stream_key, 6), axis_at), (shards_of,), jnp.float32, least / len(pieces), largest / len(pieces))
        loudness = loudness * jnp.repeat(jnp.exp(heights), extent[axis_at] // shards_of).reshape((-1,) + (1,) * (len(extent) - 1 - axis_at))
    return loudness


def normal_values(stream_key, extent, width, limit, shards=(), kind=jnp.bfloat16):
    entries = jax.random.normal(stream_key, extent, jnp.float32) * width
    if len(shards) > 0:
        entries = block_levels(stream_key, extent, shards, -0.22, 0.18) * entries
    return jnp.clip(entries, min=-limit, max=limit).astype(kind)


def setup_inputs(seed: int = 0) -> dict:
    arg_keys = jax.random.split(jax.random.key(seed), 6)
    return {
        "features": normal_values(arg_keys[0], (SCENES, N_TILE * CAP, 64, C), 1.0, 6.0, ((0, 6), (1, 128))),
        "cotangent": normal_values(arg_keys[1], (SCENES, N_TILE * CAP, 64, C), 1.0, 6.0, ((0, 6), (1, 128))),
        "blocks": draw_blocks(jax.random.fold_in(arg_keys[5], 71), 0),
        "w_first": normal_values(arg_keys[3], (27, C, C), (27 * C) ** -0.5, 0.109375),
        "w_second": normal_values(arg_keys[4], (27, C, C), (27 * C) ** -0.5, 0.109375),
    }


def build_slab(rows, slot_blocks):
    channels = rows.shape[-1]
    holder = jnp.zeros((BY * BZ + 1, 64, channels), rows.dtype).at[slot_blocks].set(rows)[: BY * BZ]
    shaped = holder.reshape(BY, BZ, 4, 4, 4, channels).transpose(2, 0, 3, 1, 4, 5)
    return shaped.reshape(4, 4 * BY, 4 * BZ, channels)


def cut_windows(padded, slot_blocks):
    channels = padded.shape[-1]
    clipped = jnp.minimum(slot_blocks, BY * BZ - 1).astype(jnp.int32)

    def single(block_id):
        anchor = jnp.zeros((), jnp.int32)
        return lax.dynamic_slice(padded, (anchor, 4 * (block_id // BZ), 4 * (block_id % BZ), anchor), (6, 6, 6, channels))

    return jax.vmap(single)(clipped)


def apply_taps(windows, weights, transposed):
    slot_count = windows.shape[0]
    channels = windows.shape[-1]
    summed = jnp.zeros((slot_count * 64, weights.shape[-1]), jnp.float32)
    for along_x in range(3):
        for along_y in range(3):
            for along_z in range(3):
                tap_index = along_x * 9 + along_y * 3 + along_z
                if transposed:
                    corner = (2 - along_x, 2 - along_y, 2 - along_z)
                    matrix = weights[tap_index].T
                else:
                    corner = (along_x, along_y, along_z)
                    matrix = weights[tap_index]
                window_piece = windows[:, corner[0]:corner[0] + 4, corner[1]:corner[1] + 4, corner[2]:corner[2] + 4, :]
                summed = summed + jnp.dot(window_piece.reshape(slot_count * 64, channels), matrix, preferred_element_type=jnp.float32)
    return summed.reshape(slot_count, 64, -1)


def weight_terms(windows, gradient):
    channels = windows.shape[-1]
    gradient_rows = gradient.reshape(-1, gradient.shape[-1])
    tap_terms = []
    for along_x in range(3):
        for along_y in range(3):
            for along_z in range(3):
                window_piece = windows[:, along_x:along_x + 4, along_y:along_y + 4, along_z:along_z + 4, :]
                tap_terms.append(lax.dot_general(window_piece.reshape(-1, channels), gradient_rows, (((0,), (0,)), ((), ())), preferred_element_type=jnp.float32))
    return jnp.stack(tap_terms)


def silu_slope(values):
    sigmoid_value = jax.nn.sigmoid(values)
    return sigmoid_value * (1.0 + values * (1.0 - sigmoid_value))


def reference(features, cotangent, blocks, w_first, w_second):
    channels = features.shape[-1]

    def scene_step(running, packed):
        feature_rows, upstream, slot_list = packed
        feature_rows = feature_rows.reshape(N_TILE, CAP, 64, channels)
        upstream = upstream.reshape(N_TILE, CAP, 64, channels)
        tile_blocks = slot_list.reshape(N_TILE, CAP)
        live_mask = (tile_blocks < BY * BZ).astype(jnp.float32)[..., None, None]
        tile_order = jnp.arange(N_TILE, dtype=jnp.int32)

        def scene_grid(rows):
            slabs = jax.vmap(build_slab)(rows, tile_blocks)
            whole = slabs.reshape(N_TILE * 4, 4 * BY, 4 * BZ, channels)
            return jnp.pad(whole, ((1, 1), (1, 1), (1, 1), (0, 0)))

        def tile_windows(grid, tile_index, slot_blocks):
            return cut_windows(lax.dynamic_slice_in_dim(grid, 4 * tile_index, 6, 0), slot_blocks)

        def run_conv(grid, weights, transposed):
            return lax.map(lambda pairing: apply_taps(tile_windows(grid, pairing[0], pairing[1]), weights, transposed), (tile_order, tile_blocks))

        input_grid = scene_grid(feature_rows)
        first_act = run_conv(input_grid, w_first, False)
        hidden = jax.nn.silu(first_act).astype(jnp.bfloat16)
        hidden_grid = scene_grid(hidden)
        second_act = run_conv(hidden_grid, w_second, False)
        output = (live_mask * (feature_rows.astype(jnp.float32) + second_act)).astype(jnp.bfloat16)
        upstream_grid = scene_grid(upstream)
        hidden_grad = run_conv(upstream_grid, w_second, True)
        first_grad = (live_mask * hidden_grad * silu_slope(first_act)).astype(jnp.bfloat16)
        masked_upstream = (upstream.astype(jnp.float32) * live_mask).astype(jnp.bfloat16)
        grad_grid = scene_grid(first_grad)
        back_conv = run_conv(grad_grid, w_first, True)
        input_out = (live_mask * (upstream.astype(jnp.float32) + back_conv)).astype(jnp.bfloat16)

        def accumulate(sums, parcel):
            tile_index, slot_blocks, grad_rows, upstream_rows = parcel
            first_sum = sums[0] + weight_terms(tile_windows(input_grid, tile_index, slot_blocks), grad_rows)
            second_sum = sums[1] + weight_terms(tile_windows(hidden_grid, tile_index, slot_blocks), upstream_rows)
            return (first_sum, second_sum), None

        running, unused = lax.scan(accumulate, running, (tile_order, tile_blocks, first_grad, masked_upstream))
        return running, (output.reshape(N_TILE * CAP, 64, channels), input_out.reshape(N_TILE * CAP, 64, channels))

    empty_sum = jnp.zeros((27, channels, channels), jnp.float32)
    totals, stacked = lax.scan(scene_step, (empty_sum, empty_sum), (features, cotangent, blocks))
    return stacked[0], stacked[1], totals[0].reshape(27, channels * channels), totals[1].reshape(27, channels * channels)
```

```python
import jax
import jax.numpy as jnp
from jax import lax
from jax.sharding import Mesh, PartitionSpec as P

BY = 2
BZ = 4
TILE = ("zh", "y", "x", "c")


def padded_2(value, sides, width):
    for axis, dim in sides:
        size, length = (lax.axis_size(axis), value.shape[dim])
        up = [(i, (i + 1) % size) for i in range(size - 1)]
        down = [(j, i) for i, j in up]
        last = lax.slice_in_dim(value, length - width, length, axis=dim)
        leading = lax.slice_in_dim(value, 0, width, axis=dim)
        before = lax.ppermute(last, axis, up)
        after = lax.ppermute(leading, axis, down)
        value = jnp.concatenate([before, value, after], axis=dim)
    return value


def build_slab(rows, slot_blocks):
    channels = rows.shape[-1]
    holder = jnp.zeros((BY * BZ + 1, 64, channels), rows.dtype).at[slot_blocks].set(rows)[: BY * BZ]
    shaped = holder.reshape(BY, BZ, 4, 4, 4, channels).transpose(2, 0, 3, 1, 4, 5)
    return shaped.reshape(4, 4 * BY, 4 * BZ, channels)


def cut_windows(padded, slot_blocks):
    channels = padded.shape[-1]
    clipped = jnp.minimum(slot_blocks, BY * BZ - 1)

    def single(block_id):
        anchor = jnp.zeros((), jnp.int32)
        return lax.dynamic_slice(
            padded, (anchor, 4 * (block_id // BZ), 4 * (block_id % BZ), anchor), (6, 6, 6, channels)
        )

    return jax.vmap(single)(clipped)


def apply_taps(windows, weights, transposed):
    slot_count = windows.shape[0]
    channels = windows.shape[-1]
    summed = jnp.zeros((slot_count * 64, weights.shape[-1]), jnp.float32)
    for along_x in range(3):
        for along_y in range(3):
            for along_z in range(3):
                tap_index = along_x * 9 + along_y * 3 + along_z
                if transposed:
                    corner = (2 - along_x, 2 - along_y, 2 - along_z)
                    matrix = weights[tap_index].T
                else:
                    corner = (along_x, along_y, along_z)
                    matrix = weights[tap_index]
                window_piece = windows[
                    :,
                    corner[0] : corner[0] + 4,
                    corner[1] : corner[1] + 4,
                    corner[2] : corner[2] + 4,
                    :,
                ]
                summed = summed + jnp.dot(
                    window_piece.reshape(slot_count * 64, channels),
                    matrix,
                    preferred_element_type=jnp.float32,
                )
    return summed.reshape(slot_count, 64, -1)


def weight_terms(windows, gradient):
    channels = windows.shape[-1]
    gradient_rows = gradient.reshape(-1, gradient.shape[-1])
    tap_terms = []
    for along_x in range(3):
        for along_y in range(3):
            for along_z in range(3):
                window_piece = windows[
                    :, along_x : along_x + 4, along_y : along_y + 4, along_z : along_z + 4, :
                ]
                tap_terms.append(
                    lax.dot_general(
                        window_piece.reshape(-1, channels),
                        gradient_rows,
                        (((0,), (0,)), ((), ())),
                        preferred_element_type=jnp.float32,
                    )
                )
    return jnp.stack(tap_terms)


def silu_slope(values):
    sigmoid_value = jax.nn.sigmoid(values)
    return sigmoid_value * (1.0 + values * (1.0 - sigmoid_value))


def pad_sides(extended):
    return jnp.pad(extended, ((0, 0), (1, 1), (1, 1), (0, 0)))


def folded(pieces):
    return pieces.astype(jnp.float32).sum(axis=0)


def summed_terms(first_terms, second_terms):
    halves = jnp.stack([first_terms, second_terms])
    parts = halves.reshape(54, 2, 8, 4, 2, 128).transpose(4, 3, 2, 1, 0, 5)
    core = lax.axis_index("c")
    kept = lax.dynamic_index_in_dim(parts, core, 0, keepdims=False)
    sent = lax.dynamic_index_in_dim(parts, 1 - core, 0, keepdims=False)
    got = lax.ppermute(sent.astype(jnp.bfloat16), "c", [(0, 1), (1, 0)])
    chip = (kept + got.astype(jnp.float32)).astype(jnp.bfloat16)
    along_x = folded(lax.all_to_all(chip, "x", 0, 0, tiled=True).reshape(4, 8, 2, 54, 128))
    along_y = folded(lax.all_to_all(along_x, "y", 0, 0, tiled=True))
    spread = jnp.broadcast_to(along_y[:, None], (2, 6, 54, 128)).reshape(12, 54, 128)
    total = folded(lax.all_to_all(spread, ("zh", "scene"), 0, 0, tiled=True))
    return total[:27], total[27:]


def on_device(features, cotangent, blocks, w_first, w_second):
    slot_blocks = blocks[0]
    inputs = features[0]
    upstream = cotangent[0]
    channels = inputs.shape[-1]
    live_mask = (slot_blocks < BY * BZ).astype(jnp.float32)[:, None, None]
    input_slab = build_slab(inputs, slot_blocks)
    upstream_slab = build_slab(upstream, slot_blocks)
    stacked_rims = padded_2(jnp.stack([input_slab, upstream_slab]), ((TILE, 1),), 1)
    input_pad = pad_sides(stacked_rims[0])
    upstream_pad = pad_sides(stacked_rims[1])
    input_windows = cut_windows(input_pad, slot_blocks)
    first_act = apply_taps(input_windows, w_first, False)
    hidden = jax.nn.silu(first_act).astype(jnp.bfloat16)
    hidden_pad = pad_sides(padded_2(build_slab(hidden, slot_blocks), ((TILE, 0),), 1))
    hidden_windows = cut_windows(hidden_pad, slot_blocks)
    second_act = apply_taps(hidden_windows, w_second, False)
    output = (live_mask * (inputs.astype(jnp.float32) + second_act)).astype(jnp.bfloat16)
    hidden_grad = apply_taps(cut_windows(upstream_pad, slot_blocks), w_second, True)
    first_grad = (live_mask * hidden_grad * silu_slope(first_act)).astype(jnp.bfloat16)
    masked_upstream = (upstream.astype(jnp.float32) * live_mask).astype(jnp.bfloat16)
    second_terms = weight_terms(hidden_windows, masked_upstream).reshape(27, channels * channels)
    grad_pad = pad_sides(padded_2(build_slab(first_grad, slot_blocks), ((TILE, 0),), 1))
    back_conv = apply_taps(cut_windows(grad_pad, slot_blocks), w_first, True)
    input_out = (live_mask * (upstream.astype(jnp.float32) + back_conv)).astype(jnp.bfloat16)
    first_terms = weight_terms(input_windows, first_grad).reshape(27, channels * channels)
    first_total, second_total = summed_terms(first_terms, second_terms)
    return (output[None], input_out[None], first_total, second_total)


def solution(mesh):
    split = Mesh(mesh.devices.reshape(2, 8, 4, 2, 6), TILE + ("scene",))
    return jax.shard_map(
        on_device,
        mesh=split,
        in_specs=(
            P("scene", TILE, None, None),
            P("scene", TILE, None, None),
            P("scene", TILE),
            P(),
            P(),
        ),
        out_specs=(
            P("scene", TILE, None, None),
            P("scene", TILE, None, None),
            P(None, TILE),
            P(None, TILE),
        ),
        check_vma=False,
    )
```

```python
import jax
import jax.numpy as jnp
from jax import lax
from jax.experimental import pallas as pl
from jax.experimental.pallas import tpu as pltpu
from jax.sharding import Mesh, PartitionSpec as P

BY = 2
BZ = 4
C = 128
SLOTS = 3
TILE = ("zh", "y", "x", "c")
SCENE = ("sa", "sb")
F32 = jnp.float32
BF16 = jnp.bfloat16


def fetch(pairs, sems):
    copies = [pltpu.make_async_copy(src, dst, sems.at[k]) for k, (src, dst) in enumerate(pairs)]
    for copy in copies:
        copy.start()
    return copies


def halo_kernel(blocks, features, cotangent, outer, inner, ids, sems):
    core = lax.axis_index("c")
    edge = pl.ds(pl.multiple_of(32 * core, 32), 32)
    copies = fetch(
        [
            (blocks, ids),
            (features.at[0, :, edge, :], outer.at[0, 0:3]),
            (cotangent.at[0, :, edge, :], outer.at[0, 3:6]),
            (features.at[0], inner.at[0:3]),
            (cotangent.at[0], inner.at[3:6]),
        ],
        sems,
    )
    copies[0].wait()
    row = lax.broadcasted_iota(jnp.int32, (32, C), 0)
    marks = jnp.zeros((32, C), F32)
    for j in range(SLOTS):
        marks = jnp.where(row == j, (ids[0, j] + 1).astype(F32), marks)
    outer[0, 6] = marks.astype(BF16)
    inner[6, 0:32] = marks.astype(BF16)
    inner[6, 32:64] = jnp.zeros((32, C), BF16)
    for copy in copies[1:]:
        copy.wait()


def block_masks(ids):
    upper = lax.broadcasted_iota(jnp.int32, (8, C), 0) // 4
    return [
        [[ids[j] == (upper + (4 * by + 2 * h)) for h in range(2)] for by in range(BY)]
        for j in range(SLOTS)
    ]


def live_tiles(masks):
    rows = []
    for by in range(BY):
        halves = []
        for h in range(2):
            any_slot = masks[0][by][h] | masks[1][by][h] | masks[2][by][h]
            halves.append(jnp.where(any_slot, 1.0, 0.0))
        tile = jnp.concatenate(halves, axis=0)
        rows.append(jnp.broadcast_to(tile[None], (4, 16, C)))
    return jnp.concatenate(rows, axis=0)


def to_slab(rows, masks, layers):
    count = SLOTS * layers * 16
    low = lax.broadcasted_iota(jnp.int32, (count, C), 0) % 8 < 4
    even = jnp.where(low, rows, pltpu.roll(rows, 4, 0))
    odd = jnp.where(low, pltpu.roll(rows, count - 4, 0), rows)
    shape = (SLOTS, layers, 2, 8, C)
    even, odd = even.reshape(shape), odd.reshape(shape)
    whole = []
    for by in range(BY):
        halves = []
        for h in range(2):
            pair = []
            for part in (even, odd):
                picked = jnp.zeros((layers, 2, 8, C), F32)
                for j in range(SLOTS):
                    picked = jnp.where(masks[j][by][h][None, None], part[j], picked)
                pair.append(picked)
            halves.append(jnp.stack(pair, axis=2).reshape(layers, 4, 8, C))
        whole.append(jnp.concatenate(halves, axis=2))
    return jnp.concatenate(whole, axis=1)


def from_slab(slab, masks, layers):
    low = lax.broadcasted_iota(jnp.int32, (8, C), 0) < 4
    slots = []
    for j in range(SLOTS):
        picked = jnp.zeros((layers, 4, 8, C), F32)
        for by in range(BY):
            for h in range(2):
                part = slab[:, 4 * by : 4 * by + 4, 8 * h : 8 * h + 8, :]
                picked = picked + jnp.where(masks[j][by][h][None, None], part, 0.0)
        flat = picked.reshape(layers * 32, C)
        both = (flat + pltpu.roll(flat, 4, 0)).reshape(layers, 2, 2, 8, C)
        rest = (flat + pltpu.roll(flat, layers * 32 - 4, 0)).reshape(layers, 2, 2, 8, C)
        full_even = rest[:, :, 0]
        full_odd = both[:, :, 1]
        slots.append(jnp.where(low[None, None], full_even, full_odd).reshape(layers * 16, C))
    return jnp.stack(slots)


def shifted_rows(slab, layers):
    flat = slab.reshape(layers * 128, C)
    z = lax.broadcasted_iota(jnp.int32, (layers * 128, C), 0) % 16
    before = jnp.where(z == 0, 0.0, pltpu.roll(flat, 1, 0))
    after = jnp.where(z == 15, 0.0, pltpu.roll(flat, layers * 128 - 1, 0))
    return before, flat, after


def store_shifted(out, slab, layers):
    for c, rows in enumerate(shifted_rows(slab, layers)):
        out[c, :, 1:9] = rows.astype(BF16).reshape(layers, 8, 16, C)
        out[c, :, 0] = jnp.zeros((layers, 16, C), BF16)
        out[c, :, 9] = jnp.zeros((layers, 16, C), BF16)


def taps(shifted, weights, layers):
    lhs = jnp.concatenate(
        [shifted[c, :, b : b + 8].reshape(layers * 128, C) for b in range(3) for c in range(3)], axis=1
    )
    rhs = jnp.concatenate([weights[9 * a : 9 * a + 9].reshape(9 * C, C) for a in range(3)], axis=1)
    return jnp.dot(lhs, rhs, preferred_element_type=F32).reshape(layers, 128, 3 * C)


def taps_back(shifted, weights, layers):
    lhs = jnp.concatenate(
        [shifted[2 - c, :, 2 - b : 10 - b].reshape(layers * 128, C) for b in range(3) for c in range(3)], axis=1
    )
    rhs = jnp.concatenate(
        [jnp.concatenate([weights[9 * (2 - a) + k] for k in range(9)], axis=1) for a in range(3)], axis=0
    )
    out = lax.dot_general(lhs, rhs, (((1,), (1,)), ((), ())), preferred_element_type=F32)
    return out.reshape(layers, 128, 3 * C)


def thirds(out):
    return out[:, :, 0:C], out[:, :, C : 2 * C], out[:, :, 2 * C : 3 * C]


def inside(out, layers):
    after, same, before = thirds(out)
    n = layers - 2
    return after[0:n] + same[1 : n + 1] + before[2 : n + 2]


def spread(out):
    after, same, before = thirds(out)
    none = jnp.zeros((1, 128, C), F32)
    return (
        jnp.concatenate([none, none, after], axis=0)
        + jnp.concatenate([none, same, none], axis=0)
        + jnp.concatenate([before, none, none], axis=0)
    )


def completed(part, out):
    after, same, before = thirds(out)
    return jnp.concatenate(
        [
            part[0:1] + after[0:1] + same[1:2],
            part[1:2] + after[1:2],
            part[2:8],
            part[8:9] + before[2:3],
            part[9:10] + same[2:3] + before[3:4],
        ],
        axis=0,
    )


def weight_terms(order, shifted_layers, padded, terms):
    turned = jnp.concatenate(
        [
            lax.dot_general(order, rows, (((1,), (1,)), ((), ())), preferred_element_type=F32).astype(BF16)
            for rows in shifted_layers
        ],
        axis=0,
    )
    rhs = jnp.concatenate([padded(a, b) for a in range(3) for b in range(3)], axis=1)
    out = jnp.dot(turned, rhs, preferred_element_type=F32)
    for a in range(3):
        for b in range(3):
            for c in range(3):
                piece = out[c * C : (c + 1) * C, (3 * a + b) * C : (3 * a + b + 1) * C]
                half, tap = divmod(9 * a + 3 * b + c, 14)
                terms[:, half, tap] = piece.astype(BF16).reshape(4, 32, C)
    terms[:, 1, 13] = jnp.zeros((4, 32, C), BF16)


def pad_store(out, slab):
    out[0:2] = jnp.zeros((2, 10, 16, C), BF16)
    out[10:12] = jnp.zeros((2, 10, 16, C), BF16)
    out[2:10, 0] = jnp.zeros((8, 16, C), BF16)
    out[2:10, 9] = jnp.zeros((8, 16, C), BF16)
    out[2:10, 1:9] = slab.astype(BF16)


def ids_of(tile):
    rows = tile.astype(F32).astype(jnp.int32)
    return [jnp.broadcast_to(rows[j : j + 1] - 1, (8, C)) for j in range(SLOTS)]


def choose(even, one, other):
    return [jnp.where(even, p, q) for p, q in zip(one, other)]


def chip_ids(own, partner, even):
    own, partner = ids_of(own[6, 0:16]), ids_of(partner[6, 0:16])
    return choose(even, own, partner), choose(even, partner, own)


def chip_kernel(
    own, partner, w_first_hbm, w_second_hbm,
    w_first, w_second, field_z, upstream_pad, act_part, grad_part,
    upstream_z, sems,
):
    copies = fetch([(w_first_hbm, w_first), (w_second_hbm, w_second)], sems)
    even = lax.axis_index("c") == 0
    masks = [block_masks(ids) for ids in chip_ids(own, partner, even)]

    def field(which):
        partner_rows = partner[3 * which : 3 * which + 3].astype(F32).reshape(192, C)
        own_rows = own[3 * which : 3 * which + 3].astype(F32).reshape(192, C)
        parts = (
            to_slab(jnp.where(even, own_rows, partner_rows), masks[0], 4),
            to_slab(jnp.where(even, partner_rows, own_rows), masks[1], 4),
        )
        return jnp.concatenate(parts, axis=0)

    store_shifted(field_z, field(0), 8)
    upstream = field(1)
    store_shifted(upstream_z, upstream, 8)
    pad_store(upstream_pad, upstream)
    copies[0].wait()
    act_part[...] = spread(taps(field_z, w_first, 8))
    copies[1].wait()
    grad_part[...] = spread(taps_back(upstream_z, w_second, 8))


def main_kernel(
    own, partner, far, near, w_first, w_second, field_z, upstream_pad, act_part, grad_part,
    terms, hidden_out, grad_out,
    outer_z, outer_up_z, stage_z, padded,
):
    core = lax.axis_index("c")
    even = core == 0
    near_ids, far_ids = ids_of(near[0, 6, 0:16]), ids_of(far[0, 6, 0:16])
    left, right = (block_masks(ids) for ids in (choose(even, near_ids, far_ids), choose(even, far_ids, near_ids)))
    lower, upper = (block_masks(ids) for ids in chip_ids(own, partner, even))

    def field(which):
        near_rows = near[0, 3 * which : 3 * which + 3].astype(F32).reshape(96, C)
        far_rows = far[0, 3 * which : 3 * which + 3].astype(F32).reshape(96, C)
        parts = (
            to_slab(jnp.where(even, near_rows, far_rows), left, 2),
            to_slab(jnp.where(even, far_rows, near_rows), right, 2),
        )
        return jnp.concatenate(parts, axis=0)

    store_shifted(outer_z, field(0), 4)
    store_shifted(outer_up_z, field(1), 4)
    first_act = completed(act_part[...], taps(outer_z, w_first, 4)).reshape(10, 8, 16, C)
    live = jnp.concatenate(
        [
            live_tiles(left)[None],
            jnp.broadcast_to(live_tiles(lower)[None], (4, 8, 16, C)),
            jnp.broadcast_to(live_tiles(upper)[None], (4, 8, 16, C)),
            live_tiles(right)[None],
        ],
        axis=0,
    )
    gate = 1.0 / (1.0 + jnp.exp(-first_act))
    hidden = live * (first_act * gate)
    hidden_out[...] = hidden.astype(BF16)
    slope = live * (gate * (1.0 + first_act * (1.0 - gate)))
    hidden_grad = completed(grad_part[...], taps_back(outer_up_z, w_second, 4)).reshape(10, 8, 16, C)
    grad_out[...] = (hidden_grad * slope).astype(BF16)

    @pl.when(even)
    def _():
        for c in range(3):
            stage_z[c, 0] = outer_z[c, 1, 1:9]
            stage_z[c, 1:9] = field_z[c, :, 1:9]
            stage_z[c, 9] = outer_z[c, 2, 1:9]
        pad_store(padded, grad_out[1:9])

    @pl.when(core == 1)
    def _():
        for c, rows in enumerate(shifted_rows(hidden_out[...].astype(F32), 10)):
            stage_z[c] = rows.astype(BF16).reshape(10, 8, 16, C)
        padded[...] = upstream_pad[...]

    r = lax.broadcasted_iota(jnp.int32, (C, C), 0)
    i = lax.broadcasted_iota(jnp.int32, (C, C), 1)
    wanted = (((r // 2) % 2 * 8 + (r // 4) % 8) * 4 + r // 32) * 2 + r % 2
    order = jnp.where(i == wanted, 1.0, 0.0).astype(BF16)
    weight_terms(
        order,
        [stage_z[c].reshape(1280, C) for c in range(3)],
        lambda a, b: padded[2 - a : 12 - a, 2 - b : 10 - b].reshape(1280, C),
        terms,
    )


def output_kernel(
    blocks, features, cotangent, hidden, first_grad, w_first, w_second,
    block_out, input_grad,
    hidden_z, grad_z,
):
    mine = pl.ds(4 * lax.axis_index("c"), 6)
    own = block_masks([blocks[0, j] for j in range(SLOTS)])
    store_shifted(hidden_z, hidden[mine].astype(F32), 6)
    store_shifted(grad_z, first_grad[mine].astype(F32), 6)
    second_act = from_slab(inside(taps(hidden_z, w_second, 6), 6).reshape(4, 8, 16, C), own, 4)
    back = from_slab(inside(taps_back(grad_z, w_first, 6), 6).reshape(4, 8, 16, C), own, 4)
    for j in range(SLOTS):
        live = jnp.where(blocks[0, j] < BY * BZ, 1.0, 0.0)
        block_out[0, j] = (live * (features[0, j].astype(F32) + second_act[j])).astype(BF16)
        input_grad[0, j] = (live * (cotangent[0, j].astype(F32) + back[j])).astype(BF16)


VMEM = pl.BlockSpec(memory_space=pltpu.VMEM)
SMEM = pl.BlockSpec(memory_space=pltpu.SMEM)
HBM = pl.BlockSpec(memory_space=pltpu.HBM)


def kernel_call(body, ins, outs, scratch, flops, room=50):
    return pl.pallas_call(
        body,
        out_shape=outs,
        in_specs=ins,
        out_specs=[VMEM] * len(outs),
        scratch_shapes=scratch,
        compiler_params=pltpu.CompilerParams(vmem_limit_bytes=room * 1024 * 1024),
        cost_estimate=pl.CostEstimate(flops=flops, bytes_accessed=4_000_000, transcendentals=0),
    )


def shape(*dims, dtype=BF16):
    return jax.ShapeDtypeStruct(dims, dtype)


def folded(pieces):
    return pieces.astype(F32).sum(axis=0)


def on_device(features, cotangent, blocks, w_first, w_second):
    outer, inner = kernel_call(
        halo_kernel,
        [HBM] * 3,
        [shape(1, 7, 32, C), shape(7, 64, C)],
        [pltpu.SMEM((1, SLOTS), jnp.int32), pltpu.SemaphoreType.DMA((5,))],
        1,
        64,
    )(blocks, features, cotangent)
    odd = range(1, 127, 2)
    partner = lax.ppermute(inner, "c", [(0, 1), (1, 0)])
    far = lax.ppermute(outer, TILE, [(t + 2, t) for t in range(0, 126, 2)] + [(t, t + 2) for t in range(1, 126, 2)])
    near = lax.ppermute(outer, TILE, [(t, t + 1) for t in odd] + [(t + 1, t) for t in odd])
    w_first, w_second, field_z, upstream_pad, act_part, grad_part = kernel_call(
        chip_kernel,
        [VMEM, VMEM, HBM, HBM],
        [
            shape(27, C, C),
            shape(27, C, C),
            shape(3, 8, 10, 16, C),
            shape(12, 10, 16, C),
            shape(10, 128, C, dtype=F32),
            shape(10, 128, C, dtype=F32),
        ],
        [pltpu.VMEM((3, 8, 10, 16, C), BF16), pltpu.SemaphoreType.DMA((2,))],
        2_000_000_000,
        40,
    )(inner, partner, w_first, w_second)
    terms, hidden, first_grad = kernel_call(
        main_kernel,
        [VMEM] * 10,
        [shape(4, 2, 14, 32, C), shape(10, 8, 16, C), shape(10, 8, 16, C)],
        [
            pltpu.VMEM((3, 4, 10, 16, C), BF16),
            pltpu.VMEM((3, 4, 10, 16, C), BF16),
            pltpu.VMEM((3, 10, 8, 16, C), BF16),
            pltpu.VMEM((12, 10, 16, C), BF16),
        ],
        2_000_000_000,
        40,
    )(inner, partner, far, near, w_first, w_second, field_z, upstream_pad, act_part, grad_part)
    block_out, input_grad = kernel_call(
        output_kernel,
        [SMEM] + [VMEM] * 6,
        [shape(1, SLOTS, 64, C)] * 2,
        [pltpu.VMEM((3, 6, 10, 16, C), BF16), pltpu.VMEM((3, 6, 10, 16, C), BF16)],
        1_400_000_000,
    )(blocks, features, cotangent, hidden, first_grad, w_first, w_second)
    terms = terms.reshape(8, 14, 32, C)
    along_x = folded(lax.all_to_all(terms, ("x", "sb"), 0, 0, tiled=True)).reshape(14, 8, 4, C)
    along_y = folded(lax.all_to_all(along_x.transpose(1, 2, 0, 3), "y", 0, 0, tiled=True)).astype(BF16)
    copies = jnp.broadcast_to(along_y[:, None], (4, 6, 14, C)).reshape(24, 14, C)
    pieces = lax.all_to_all(copies, ("zh", "c", "sa", "sb"), 0, 0, tiled=True).reshape(2, 2, 3, 2, 14, C)
    total = pieces.astype(F32).sum(axis=(0, 2)).reshape(2, 28, C)
    return block_out, input_grad, total[0, :27], total[1, :27]


def solution(mesh):
    split = Mesh(mesh.devices.reshape(2, 8, 4, 2, 3, 2), TILE + SCENE)
    return jax.shard_map(
        on_device,
        mesh=split,
        in_specs=(
            P(SCENE, TILE, None, None),
            P(SCENE, TILE, None, None),
            P(SCENE, TILE),
            P(),
            P(),
        ),
        out_specs=(
            P(SCENE, TILE, None, None),
            P(SCENE, TILE, None, None),
            P(None, TILE),
            P(None, TILE),
        ),
        check_vma=False,
    )
```

```python
import jax
import jax.numpy as jnp
from jax import lax
from jax.experimental import pallas as pl
from jax.experimental.pallas import tpu as pltpu
from jax.sharding import Mesh, PartitionSpec as P

BY = 2
BZ = 4
C = 128
SLOTS = 3
TILE = ("zh", "y", "x", "c")
SCENE = ("sa", "sb")
F32 = jnp.float32
BF16 = jnp.bfloat16


def fetch(pairs, sems):
    copies = [pltpu.make_async_copy(src, dst, sems.at[k]) for k, (src, dst) in enumerate(pairs)]
    for copy in copies:
        copy.start()
    return copies


def halo_kernel(blocks, features, cotangent, outer, inner, ids, sems):
    core = lax.axis_index("c")
    edge = pl.ds(pl.multiple_of(32 * core, 32), 32)
    copies = fetch(
        [
            (blocks, ids),
            (features.at[0, :, edge, :], outer.at[0, 0:3]),
            (cotangent.at[0, :, edge, :], outer.at[0, 3:6]),
            (features.at[0], inner.at[0:3]),
            (cotangent.at[0], inner.at[3:6]),
        ],
        sems,
    )
    copies[0].wait()
    row = lax.broadcasted_iota(jnp.int32, (32, C), 0)
    marks = jnp.zeros((32, C), F32)
    for j in range(SLOTS):
        marks = jnp.where(row == j, (ids[0, j] + 1).astype(F32), marks)
    outer[0, 6] = marks.astype(BF16)
    inner[6, 0:32] = marks.astype(BF16)
    inner[6, 32:64] = jnp.zeros((32, C), BF16)
    for copy in copies[1:]:
        copy.wait()


def block_masks(ids):
    upper = lax.broadcasted_iota(jnp.int32, (8, C), 0) // 4
    return [
        [[ids[j] == (upper + (4 * by + 2 * h)) for h in range(2)] for by in range(BY)]
        for j in range(SLOTS)
    ]


def live_tiles(masks):
    rows = []
    for by in range(BY):
        halves = []
        for h in range(2):
            any_slot = masks[0][by][h] | masks[1][by][h] | masks[2][by][h]
            halves.append(jnp.where(any_slot, 1.0, 0.0))
        tile = jnp.concatenate(halves, axis=0)
        rows.append(jnp.broadcast_to(tile[None], (4, 16, C)))
    return jnp.concatenate(rows, axis=0)


def to_slab(rows, masks, layers):
    count = SLOTS * layers * 16
    low = lax.broadcasted_iota(jnp.int32, (count, C), 0) % 8 < 4
    even = jnp.where(low, rows, pltpu.roll(rows, 4, 0))
    odd = jnp.where(low, pltpu.roll(rows, count - 4, 0), rows)
    shape = (SLOTS, layers, 2, 8, C)
    even, odd = even.reshape(shape), odd.reshape(shape)
    whole = []
    for by in range(BY):
        halves = []
        for h in range(2):
            pair = []
            for part in (even, odd):
                picked = jnp.zeros((layers, 2, 8, C), F32)
                for j in range(SLOTS):
                    picked = jnp.where(masks[j][by][h][None, None], part[j], picked)
                pair.append(picked)
            halves.append(jnp.stack(pair, axis=2).reshape(layers, 4, 8, C))
        whole.append(jnp.concatenate(halves, axis=2))
    return jnp.concatenate(whole, axis=1)


def from_slab(slab, masks, layers):
    low = lax.broadcasted_iota(jnp.int32, (8, C), 0) < 4
    slots = []
    for j in range(SLOTS):
        picked = jnp.zeros((layers, 4, 8, C), F32)
        for by in range(BY):
            for h in range(2):
                part = slab[:, 4 * by : 4 * by + 4, 8 * h : 8 * h + 8, :]
                picked = picked + jnp.where(masks[j][by][h][None, None], part, 0.0)
        flat = picked.reshape(layers * 32, C)
        both = (flat + pltpu.roll(flat, 4, 0)).reshape(layers, 2, 2, 8, C)
        rest = (flat + pltpu.roll(flat, layers * 32 - 4, 0)).reshape(layers, 2, 2, 8, C)
        full_even = rest[:, :, 0]
        full_odd = both[:, :, 1]
        slots.append(jnp.where(low[None, None], full_even, full_odd).reshape(layers * 16, C))
    return jnp.stack(slots)


def shifted_rows(slab, layers):
    flat = slab.reshape(layers * 128, C)
    z = lax.broadcasted_iota(jnp.int32, (layers * 128, C), 0) % 16
    before = jnp.where(z == 0, 0.0, pltpu.roll(flat, 1, 0))
    after = jnp.where(z == 15, 0.0, pltpu.roll(flat, layers * 128 - 1, 0))
    return before, flat, after


def store_shifted(out, slab, layers):
    for c, rows in enumerate(shifted_rows(slab, layers)):
        out[c, :, 1:9] = rows.astype(BF16).reshape(layers, 8, 16, C)
        out[c, :, 0] = jnp.zeros((layers, 16, C), BF16)
        out[c, :, 9] = jnp.zeros((layers, 16, C), BF16)


def taps(shifted, weights, layers):
    lhs = jnp.concatenate(
        [shifted[c, :, b : b + 8].reshape(layers * 128, C) for b in range(3) for c in range(3)], axis=1
    )
    rhs = jnp.concatenate([weights[9 * a : 9 * a + 9].reshape(9 * C, C) for a in range(3)], axis=1)
    return jnp.dot(lhs, rhs, preferred_element_type=F32).reshape(layers, 128, 3 * C)


def taps_back(shifted, weights, layers):
    lhs = jnp.concatenate(
        [shifted[2 - c, :, 2 - b : 10 - b].reshape(layers * 128, C) for b in range(3) for c in range(3)], axis=1
    )
    rhs = jnp.concatenate(
        [jnp.concatenate([weights[9 * (2 - a) + k] for k in range(9)], axis=1) for a in range(3)], axis=0
    )
    out = lax.dot_general(lhs, rhs, (((1,), (1,)), ((), ())), preferred_element_type=F32)
    return out.reshape(layers, 128, 3 * C)


def thirds(out):
    return out[:, :, 0:C], out[:, :, C : 2 * C], out[:, :, 2 * C : 3 * C]


def inside(out, layers):
    after, same, before = thirds(out)
    n = layers - 2
    return after[0:n] + same[1 : n + 1] + before[2 : n + 2]


def spread(out):
    after, same, before = thirds(out)
    none = jnp.zeros((1, 128, C), F32)
    return (
        jnp.concatenate([none, none, after], axis=0)
        + jnp.concatenate([none, same, none], axis=0)
        + jnp.concatenate([before, none, none], axis=0)
    )


def completed(part, out):
    after, same, before = thirds(out)
    return jnp.concatenate(
        [
            part[0:1] + after[0:1] + same[1:2],
            part[1:2] + after[1:2],
            part[2:8],
            part[8:9] + before[2:3],
            part[9:10] + same[2:3] + before[3:4],
        ],
        axis=0,
    )


def weight_terms(order, shifted_layers, padded, terms):
    turned = jnp.concatenate(
        [
            lax.dot_general(order, rows, (((1,), (1,)), ((), ())), preferred_element_type=F32).astype(BF16)
            for rows in shifted_layers
        ],
        axis=0,
    )
    rhs = jnp.concatenate([padded(a, b) for a in range(3) for b in range(3)], axis=1)
    out = jnp.dot(turned, rhs, preferred_element_type=F32)
    for a in range(3):
        for b in range(3):
            for c in range(3):
                piece = out[c * C : (c + 1) * C, (3 * a + b) * C : (3 * a + b + 1) * C]
                half, tap = divmod(9 * a + 3 * b + c, 14)
                terms[:, half, tap] = piece.astype(BF16).reshape(4, 32, C)
    terms[:, 1, 13] = jnp.zeros((4, 32, C), BF16)


def pad_store(out, slab):
    out[0:2] = jnp.zeros((2, 10, 16, C), BF16)
    out[10:12] = jnp.zeros((2, 10, 16, C), BF16)
    out[2:10, 0] = jnp.zeros((8, 16, C), BF16)
    out[2:10, 9] = jnp.zeros((8, 16, C), BF16)
    out[2:10, 1:9] = slab.astype(BF16)


def ids_of(tile):
    rows = tile.astype(F32).astype(jnp.int32)
    return [jnp.broadcast_to(rows[j : j + 1] - 1, (8, C)) for j in range(SLOTS)]


def choose(even, one, other):
    return [jnp.where(even, p, q) for p, q in zip(one, other)]


def chip_ids(own, partner, even):
    own, partner = ids_of(own[6, 0:16]), ids_of(partner[6, 0:16])
    return choose(even, own, partner), choose(even, partner, own)


def chip_kernel(
    own, partner, w_first_hbm, w_second_hbm,
    w_first, w_second, field_z, upstream_pad, act_part, grad_part,
    upstream_z, sems,
):
    copies = fetch([(w_first_hbm, w_first), (w_second_hbm, w_second)], sems)
    even = lax.axis_index("c") == 0
    masks = [block_masks(ids) for ids in chip_ids(own, partner, even)]

    def field(which):
        partner_rows = partner[3 * which : 3 * which + 3].astype(F32).reshape(192, C)
        own_rows = own[3 * which : 3 * which + 3].astype(F32).reshape(192, C)
        parts = (
            to_slab(jnp.where(even, own_rows, partner_rows), masks[0], 4),
            to_slab(jnp.where(even, partner_rows, own_rows), masks[1], 4),
        )
        return jnp.concatenate(parts, axis=0)

    store_shifted(field_z, field(0), 8)
    upstream = field(1)
    store_shifted(upstream_z, upstream, 8)
    pad_store(upstream_pad, upstream)
    copies[0].wait()
    act_part[...] = spread(taps(field_z, w_first, 8))
    copies[1].wait()
    grad_part[...] = spread(taps_back(upstream_z, w_second, 8))


def main_kernel(
    own, partner, far, near, w_first, w_second, field_z, upstream_pad, act_part, grad_part,
    terms, hidden_out, grad_out,
    outer_z, outer_up_z, stage_z, padded,
):
    core = lax.axis_index("c")
    even = core == 0
    near_ids, far_ids = ids_of(near[0, 6, 0:16]), ids_of(far[0, 6, 0:16])
    left, right = (block_masks(ids) for ids in (choose(even, near_ids, far_ids), choose(even, far_ids, near_ids)))
    lower, upper = (block_masks(ids) for ids in chip_ids(own, partner, even))

    def field(which):
        near_rows = near[0, 3 * which : 3 * which + 3].astype(F32).reshape(96, C)
        far_rows = far[0, 3 * which : 3 * which + 3].astype(F32).reshape(96, C)
        parts = (
            to_slab(jnp.where(even, near_rows, far_rows), left, 2),
            to_slab(jnp.where(even, far_rows, near_rows), right, 2),
        )
        return jnp.concatenate(parts, axis=0)

    store_shifted(outer_z, field(0), 4)
    store_shifted(outer_up_z, field(1), 4)
    first_act = completed(act_part[...], taps(outer_z, w_first, 4)).reshape(10, 8, 16, C)
    live = jnp.concatenate(
        [
            live_tiles(left)[None],
            jnp.broadcast_to(live_tiles(lower)[None], (4, 8, 16, C)),
            jnp.broadcast_to(live_tiles(upper)[None], (4, 8, 16, C)),
            live_tiles(right)[None],
        ],
        axis=0,
    )
    gate = 1.0 / (1.0 + jnp.exp(-first_act))
    hidden = live * (first_act * gate)
    hidden_out[...] = hidden.astype(BF16)
    slope = live * (gate * (1.0 + first_act * (1.0 - gate)))
    hidden_grad = completed(grad_part[...], taps_back(outer_up_z, w_second, 4)).reshape(10, 8, 16, C)
    grad_out[...] = (hidden_grad * slope).astype(BF16)

    @pl.when(even)
    def _():
        for c in range(3):
            stage_z[c, 0] = outer_z[c, 1, 1:9]
            stage_z[c, 1:9] = field_z[c, :, 1:9]
            stage_z[c, 9] = outer_z[c, 2, 1:9]
        pad_store(padded, grad_out[1:9])

    @pl.when(core == 1)
    def _():
        for c, rows in enumerate(shifted_rows(hidden_out[...].astype(F32), 10)):
            stage_z[c] = rows.astype(BF16).reshape(10, 8, 16, C)
        padded[...] = upstream_pad[...]

    r = lax.broadcasted_iota(jnp.int32, (C, C), 0)
    i = lax.broadcasted_iota(jnp.int32, (C, C), 1)
    wanted = (((r // 2) % 2 * 8 + (r // 4) % 8) * 4 + r // 32) * 2 + r % 2
    order = jnp.where(i == wanted, 1.0, 0.0).astype(BF16)
    weight_terms(
        order,
        [stage_z[c].reshape(1280, C) for c in range(3)],
        lambda a, b: padded[2 - a : 12 - a, 2 - b : 10 - b].reshape(1280, C),
        terms,
    )


def output_kernel(
    blocks, features, cotangent, hidden, first_grad, w_first, w_second,
    block_out, input_grad,
    hidden_z, grad_z,
):
    mine = pl.ds(4 * lax.axis_index("c"), 6)
    own = block_masks([blocks[0, j] for j in range(SLOTS)])
    store_shifted(hidden_z, hidden[mine].astype(F32), 6)
    store_shifted(grad_z, first_grad[mine].astype(F32), 6)
    second_act = from_slab(inside(taps(hidden_z, w_second, 6), 6).reshape(4, 8, 16, C), own, 4)
    back = from_slab(inside(taps_back(grad_z, w_first, 6), 6).reshape(4, 8, 16, C), own, 4)
    for j in range(SLOTS):
        live = jnp.where(blocks[0, j] < BY * BZ, 1.0, 0.0)
        block_out[0, j] = (live * (features[0, j].astype(F32) + second_act[j])).astype(BF16)
        input_grad[0, j] = (live * (cotangent[0, j].astype(F32) + back[j])).astype(BF16)


VMEM = pl.BlockSpec(memory_space=pltpu.VMEM)
SMEM = pl.BlockSpec(memory_space=pltpu.SMEM)
HBM = pl.BlockSpec(memory_space=pltpu.HBM)


def kernel_call(body, ins, outs, scratch, flops, room=50):
    return pl.pallas_call(
        body,
        out_shape=outs,
        in_specs=ins,
        out_specs=[VMEM] * len(outs),
        scratch_shapes=scratch,
        compiler_params=pltpu.CompilerParams(vmem_limit_bytes=room * 1024 * 1024),
        cost_estimate=pl.CostEstimate(flops=flops, bytes_accessed=4_000_000, transcendentals=0),
    )


def in_hbm(*arrays):
    return [pltpu.with_memory_space_constraint(a, pltpu.HBM) for a in arrays]


def shape(*dims, dtype=BF16):
    return jax.ShapeDtypeStruct(dims, dtype)


def folded(pieces):
    return pieces.astype(F32).sum(axis=0)


def on_device(features, cotangent, blocks, w_first, w_second):
    outer, inner = kernel_call(
        halo_kernel,
        [HBM] * 3,
        [shape(1, 7, 32, C), shape(7, 64, C)],
        [pltpu.SMEM((1, SLOTS), jnp.int32), pltpu.SemaphoreType.DMA((5,))],
        1,
        40,
    )(*in_hbm(blocks, features, cotangent))
    odd = range(1, 127, 2)
    partner = lax.ppermute(inner, "c", [(0, 1), (1, 0)])
    far = lax.ppermute(outer, TILE, [(t + 2, t) for t in range(0, 126, 2)] + [(t, t + 2) for t in range(1, 126, 2)])
    near = lax.ppermute(outer, TILE, [(t, t + 1) for t in odd] + [(t + 1, t) for t in odd])
    w_first, w_second, field_z, upstream_pad, act_part, grad_part = kernel_call(
        chip_kernel,
        [VMEM, VMEM, HBM, HBM],
        [
            shape(27, C, C),
            shape(27, C, C),
            shape(3, 8, 10, 16, C),
            shape(12, 10, 16, C),
            shape(10, 128, C, dtype=F32),
            shape(10, 128, C, dtype=F32),
        ],
        [pltpu.VMEM((3, 8, 10, 16, C), BF16), pltpu.SemaphoreType.DMA((2,))],
        2_000_000_000,
        40,
    )(inner, partner, *in_hbm(w_first, w_second))
    terms, hidden, first_grad = kernel_call(
        main_kernel,
        [VMEM] * 10,
        [shape(4, 2, 14, 32, C), shape(10, 8, 16, C), shape(10, 8, 16, C)],
        [
            pltpu.VMEM((3, 4, 10, 16, C), BF16),
            pltpu.VMEM((3, 4, 10, 16, C), BF16),
            pltpu.VMEM((3, 10, 8, 16, C), BF16),
            pltpu.VMEM((12, 10, 16, C), BF16),
        ],
        2_000_000_000,
        40,
    )(inner, partner, far, near, w_first, w_second, field_z, upstream_pad, act_part, grad_part)
    block_out, input_grad = kernel_call(
        output_kernel,
        [SMEM] + [VMEM] * 6,
        [shape(1, SLOTS, 64, C)] * 2,
        [pltpu.VMEM((3, 6, 10, 16, C), BF16), pltpu.VMEM((3, 6, 10, 16, C), BF16)],
        1_400_000_000,
    )(blocks, features, cotangent, hidden, first_grad, w_first, w_second)
    terms = terms.reshape(8, 14, 32, C)
    along_x = folded(lax.all_to_all(terms, ("x", "sb"), 0, 0, tiled=True)).reshape(14, 8, 4, C)
    along_y = folded(lax.all_to_all(along_x.transpose(1, 2, 0, 3), "y", 0, 0, tiled=True)).astype(BF16)
    copies = jnp.broadcast_to(along_y[:, None], (4, 6, 14, C)).reshape(24, 14, C)
    pieces = lax.all_to_all(copies, ("zh", "c", "sa", "sb"), 0, 0, tiled=True).reshape(2, 2, 3, 2, 14, C)
    total = pieces.astype(F32).sum(axis=(0, 2)).reshape(2, 28, C)
    return block_out, input_grad, total[0, :27], total[1, :27]


def solution(mesh):
    split = Mesh(mesh.devices.reshape(2, 8, 4, 2, 3, 2), TILE + SCENE)
    return jax.shard_map(
        on_device,
        mesh=split,
        in_specs=(
            P(SCENE, TILE, None, None),
            P(SCENE, TILE, None, None),
            P(SCENE, TILE),
            P(),
            P(),
        ),
        out_specs=(
            P(SCENE, TILE, None, None),
            P(SCENE, TILE, None, None),
            P(None, TILE),
            P(None, TILE),
        ),
        check_vma=False,
    )
```

```python
import jax
import jax.numpy as jnp
from jax import lax
from jax.experimental import pallas as pl
from jax.experimental.pallas import tpu as pltpu
from jax.sharding import Mesh, PartitionSpec as P

BY = 2
BZ = 4
C = 128
SLOTS = 3
TILE = ("zh", "y", "x", "c")
SCENE = ("sa", "sb")
F32 = jnp.float32
BF16 = jnp.bfloat16


def fetch(pairs, sems, first=0):
    copies = [pltpu.make_async_copy(src, dst, sems.at[first + k]) for k, (src, dst) in enumerate(pairs)]
    for copy in copies:
        copy.start()
    return copies


def halo_kernel(blocks, features, cotangent, outer, inner, ids, sems):
    core = lax.axis_index("c")
    edge = pl.ds(pl.multiple_of(32 * core, 32), 32)
    copies = fetch(
        [
            (blocks, ids),
            (features.at[0, :, edge, :], outer.at[0, 0:3]),
            (cotangent.at[0, :, edge, :], outer.at[0, 3:6]),
            (features.at[0], inner.at[0:3]),
            (cotangent.at[0], inner.at[3:6]),
        ],
        sems,
    )
    copies[0].wait()
    row = lax.broadcasted_iota(jnp.int32, (32, C), 0)
    marks = jnp.zeros((32, C), F32)
    for j in range(SLOTS):
        marks = jnp.where(row == j, (ids[0, j] + 1).astype(F32), marks)
    outer[0, 6] = marks.astype(BF16)
    inner[6, 0:32] = marks.astype(BF16)
    inner[6, 32:64] = jnp.zeros((32, C), BF16)
    for copy in copies[1:]:
        copy.wait()


def block_masks(ids):
    upper = lax.broadcasted_iota(jnp.int32, (8, C), 0) // 4
    return [
        [[ids[j] == (upper + (4 * by + 2 * h)) for h in range(2)] for by in range(BY)]
        for j in range(SLOTS)
    ]


def live_tiles(masks):
    rows = []
    for by in range(BY):
        halves = []
        for h in range(2):
            any_slot = masks[0][by][h] | masks[1][by][h] | masks[2][by][h]
            halves.append(jnp.where(any_slot, 1.0, 0.0))
        tile = jnp.concatenate(halves, axis=0)
        rows.append(jnp.broadcast_to(tile[None], (4, 16, C)))
    return jnp.concatenate(rows, axis=0)


def to_slab(rows, masks, layers):
    count = SLOTS * layers * 16
    low = lax.broadcasted_iota(jnp.int32, (count, C), 0) % 8 < 4
    even = jnp.where(low, rows, pltpu.roll(rows, 4, 0))
    odd = jnp.where(low, pltpu.roll(rows, count - 4, 0), rows)
    shape = (SLOTS, layers, 2, 8, C)
    even, odd = even.reshape(shape), odd.reshape(shape)
    whole = []
    for by in range(BY):
        halves = []
        for h in range(2):
            pair = []
            for part in (even, odd):
                picked = jnp.zeros((layers, 2, 8, C), F32)
                for j in range(SLOTS):
                    picked = jnp.where(masks[j][by][h][None, None], part[j], picked)
                pair.append(picked)
            halves.append(jnp.stack(pair, axis=2).reshape(layers, 4, 8, C))
        whole.append(jnp.concatenate(halves, axis=2))
    return jnp.concatenate(whole, axis=1)


def from_slab(slab, masks, layers):
    low = lax.broadcasted_iota(jnp.int32, (8, C), 0) < 4
    slots = []
    for j in range(SLOTS):
        picked = jnp.zeros((layers, 4, 8, C), F32)
        for by in range(BY):
            for h in range(2):
                part = slab[:, 4 * by : 4 * by + 4, 8 * h : 8 * h + 8, :]
                picked = picked + jnp.where(masks[j][by][h][None, None], part, 0.0)
        flat = picked.reshape(layers * 32, C)
        both = (flat + pltpu.roll(flat, 4, 0)).reshape(layers, 2, 2, 8, C)
        rest = (flat + pltpu.roll(flat, layers * 32 - 4, 0)).reshape(layers, 2, 2, 8, C)
        full_even = rest[:, :, 0]
        full_odd = both[:, :, 1]
        slots.append(jnp.where(low[None, None], full_even, full_odd).reshape(layers * 16, C))
    return jnp.stack(slots)


def shifted_rows(slab, layers):
    flat = slab.reshape(layers * 128, C)
    z = lax.broadcasted_iota(jnp.int32, (layers * 128, C), 0) % 16
    before = jnp.where(z == 0, 0.0, pltpu.roll(flat, 1, 0))
    after = jnp.where(z == 15, 0.0, pltpu.roll(flat, layers * 128 - 1, 0))
    return before, flat, after


def store_shifted(out, slab, layers):
    for c, rows in enumerate(shifted_rows(slab, layers)):
        out[c, :, 1:9] = rows.astype(BF16).reshape(layers, 8, 16, C)
        out[c, :, 0] = jnp.zeros((layers, 16, C), BF16)
        out[c, :, 9] = jnp.zeros((layers, 16, C), BF16)


def patches(shifted, first, layers, back):
    rows = pl.ds(first, layers)
    return [
        (shifted[2 - c, rows, 2 - b : 10 - b] if back else shifted[c, rows, b : b + 8]).reshape(layers * 128, C)
        for b in range(3)
        for c in range(3)
    ]


def matrices(weights, k, back):
    return [weights[9 * (2 - k if back else k) + j] for j in range(9)]


def product(pieces, columns, layers, back):
    lhs = jnp.concatenate(pieces, axis=1)
    rhs = jnp.concatenate([jnp.concatenate(col, axis=1 if back else 0) for col in columns], axis=0 if back else 1)
    out = lax.dot_general(lhs, rhs, (((1,), (1 if back else 0,)), ((), ())), preferred_element_type=F32)
    out = out.reshape(layers, 128, len(columns) * C)
    return [out[:, :, n * C : (n + 1) * C] for n in range(len(columns))]


def taps(shifted, weights, layers, back=False):
    pieces = patches(shifted, 0, layers, back)
    after, same = product(pieces, [matrices(weights, 0, back), matrices(weights, 1, back)], layers, back)
    last = matrices(weights, 2, back)
    none = jnp.zeros((C, C), BF16)
    before, aside = product(pieces[:6], [last[:6], [none] * 3 + last[6:]], layers, back)
    aside = aside.reshape(layers, 8, 16, C)
    edge = jnp.zeros((layers, 1, 16, C), F32)
    moved = [edge, aside[:, :7]] if back else [aside[:, 1:], edge]
    return after, same, before + jnp.concatenate(moved, axis=1).reshape(layers, 128, C)


def inside(out, layers):
    after, same, before = out
    n = layers - 2
    return after[0:n] + same[1 : n + 1] + before[2 : n + 2]


def spread(out):
    after, same, before = out
    none = jnp.zeros((1, 128, C), F32)
    return (
        jnp.concatenate([none, none, after], axis=0)
        + jnp.concatenate([none, same, none], axis=0)
        + jnp.concatenate([before, none, none], axis=0)
    )


def completed(part, shifted, weights, back=False):
    after, left = product(
        patches(shifted, 0, 2, back), [matrices(weights, 0, back), matrices(weights, 1, back)], 2, back
    )
    right, before = product(
        patches(shifted, 2, 2, back), [matrices(weights, 1, back), matrices(weights, 2, back)], 2, back
    )
    return jnp.concatenate(
        [
            part[0:1] + after[0:1] + left[1:2],
            part[1:2] + after[1:2],
            part[2:8],
            part[8:9] + before[0:1],
            part[9:10] + right[0:1] + before[1:2],
        ],
        axis=0,
    )


def weight_terms(order, shifted_layers, padded, terms):
    turned = jnp.concatenate(
        [
            lax.dot_general(order, rows, (((1,), (1,)), ((), ())), preferred_element_type=F32).astype(BF16)
            for rows in shifted_layers
        ],
        axis=0,
    )
    rhs = jnp.concatenate([padded(a, b) for a in range(3) for b in range(3)], axis=1)
    out = jnp.dot(turned, rhs, preferred_element_type=F32)
    for a in range(3):
        for b in range(3):
            for c in range(3):
                piece = out[c * C : (c + 1) * C, (3 * a + b) * C : (3 * a + b + 1) * C]
                half, tap = divmod(9 * a + 3 * b + c, 14)
                terms[:, half, tap] = piece.astype(BF16).reshape(4, 32, C)
    terms[:, 1, 13] = jnp.zeros((4, 32, C), BF16)


def pad_store(out, slab):
    out[0:2] = jnp.zeros((2, 10, 16, C), BF16)
    out[10:12] = jnp.zeros((2, 10, 16, C), BF16)
    out[2:10, 0] = jnp.zeros((8, 16, C), BF16)
    out[2:10, 9] = jnp.zeros((8, 16, C), BF16)
    out[2:10, 1:9] = slab.astype(BF16)


def ids_of(tile):
    rows = tile.astype(F32).astype(jnp.int32)
    return [jnp.broadcast_to(rows[j : j + 1] - 1, (8, C)) for j in range(SLOTS)]


def choose(even, one, other):
    return [jnp.where(even, p, q) for p, q in zip(one, other)]


def chip_ids(own, partner, even):
    own, partner = ids_of(own[6, 0:16]), ids_of(partner[6, 0:16])
    return choose(even, own, partner), choose(even, partner, own)


def chip_kernel(
    own, partner, w_first_hbm, w_second_hbm,
    w_first, w_second, field_z, upstream_pad, act_part, grad_part,
    upstream_z, sems,
):
    thirds = [pl.ds(9 * k, 9) for k in range(3)]
    one = fetch([(w_first_hbm.at[k], w_first.at[k]) for k in thirds], sems, 0)
    even = lax.axis_index("c") == 0
    masks = [block_masks(ids) for ids in chip_ids(own, partner, even)]

    def field(which):
        partner_rows = partner[3 * which : 3 * which + 3].astype(F32).reshape(192, C)
        own_rows = own[3 * which : 3 * which + 3].astype(F32).reshape(192, C)
        parts = (
            to_slab(jnp.where(even, own_rows, partner_rows), masks[0], 4),
            to_slab(jnp.where(even, partner_rows, own_rows), masks[1], 4),
        )
        return jnp.concatenate(parts, axis=0)

    store_shifted(field_z, field(0), 8)
    two = fetch([(w_second_hbm.at[k], w_second.at[k]) for k in thirds], sems, 3)
    upstream = field(1)
    store_shifted(upstream_z, upstream, 8)
    pad_store(upstream_pad, upstream)
    for copy in one:
        copy.wait()
    act_part[...] = spread(taps(field_z, w_first, 8))
    for copy in two:
        copy.wait()
    grad_part[...] = spread(taps(upstream_z, w_second, 8, True))


def main_kernel(
    own, partner, far, near, w_first, w_second, field_z, upstream_pad, act_part, grad_part,
    terms, hidden_out, grad_out,
    outer_z, outer_up_z, stage_z, padded,
):
    core = lax.axis_index("c")
    even = core == 0
    near_ids, far_ids = ids_of(near[0, 6, 0:16]), ids_of(far[0, 6, 0:16])
    left, right = (block_masks(ids) for ids in (choose(even, near_ids, far_ids), choose(even, far_ids, near_ids)))
    lower, upper = (block_masks(ids) for ids in chip_ids(own, partner, even))

    def field(which):
        near_rows = near[0, 3 * which : 3 * which + 3].astype(F32).reshape(96, C)
        far_rows = far[0, 3 * which : 3 * which + 3].astype(F32).reshape(96, C)
        parts = (
            to_slab(jnp.where(even, near_rows, far_rows), left, 2),
            to_slab(jnp.where(even, far_rows, near_rows), right, 2),
        )
        return jnp.concatenate(parts, axis=0)

    store_shifted(outer_z, field(0), 4)
    store_shifted(outer_up_z, field(1), 4)
    first_act = completed(act_part[...], outer_z, w_first).reshape(10, 8, 16, C)
    live = jnp.concatenate(
        [
            live_tiles(left)[None],
            jnp.broadcast_to(live_tiles(lower)[None], (4, 8, 16, C)),
            jnp.broadcast_to(live_tiles(upper)[None], (4, 8, 16, C)),
            live_tiles(right)[None],
        ],
        axis=0,
    )
    gate = 1.0 / (1.0 + jnp.exp(-first_act))
    hidden = live * (first_act * gate)
    hidden_out[...] = hidden.astype(BF16)
    slope = live * (gate * (1.0 + first_act * (1.0 - gate)))
    hidden_grad = completed(grad_part[...], outer_up_z, w_second, True).reshape(10, 8, 16, C)
    grad_out[...] = (hidden_grad * slope).astype(BF16)

    @pl.when(even)
    def _():
        for c in range(3):
            stage_z[c, 0] = outer_z[c, 1, 1:9]
            stage_z[c, 1:9] = field_z[c, :, 1:9]
            stage_z[c, 9] = outer_z[c, 2, 1:9]
        pad_store(padded, grad_out[1:9])

    @pl.when(core == 1)
    def _():
        for c, rows in enumerate(shifted_rows(hidden_out[...].astype(F32), 10)):
            stage_z[c] = rows.astype(BF16).reshape(10, 8, 16, C)
        padded[...] = upstream_pad[...]

    r = lax.broadcasted_iota(jnp.int32, (C, C), 0)
    i = lax.broadcasted_iota(jnp.int32, (C, C), 1)
    wanted = (((r // 2) % 2 * 8 + (r // 4) % 8) * 4 + r // 32) * 2 + r % 2
    order = jnp.where(i == wanted, 1.0, 0.0).astype(BF16)
    weight_terms(
        order,
        [stage_z[c].reshape(1280, C) for c in range(3)],
        lambda a, b: padded[2 - a : 12 - a, 2 - b : 10 - b].reshape(1280, C),
        terms,
    )


def output_kernel(
    blocks, features, cotangent, hidden, first_grad, w_first, w_second,
    block_out, input_grad,
    hidden_z, grad_z,
):
    mine = pl.ds(4 * lax.axis_index("c"), 6)
    own = block_masks([blocks[0, j] for j in range(SLOTS)])
    store_shifted(hidden_z, hidden[mine].astype(F32), 6)
    store_shifted(grad_z, first_grad[mine].astype(F32), 6)
    second_act = from_slab(inside(taps(hidden_z, w_second, 6), 6).reshape(4, 8, 16, C), own, 4)
    back = from_slab(inside(taps(grad_z, w_first, 6, True), 6).reshape(4, 8, 16, C), own, 4)
    for j in range(SLOTS):
        live = jnp.where(blocks[0, j] < BY * BZ, 1.0, 0.0)
        block_out[0, j] = (live * (features[0, j].astype(F32) + second_act[j])).astype(BF16)
        input_grad[0, j] = (live * (cotangent[0, j].astype(F32) + back[j])).astype(BF16)


def repeat_kernel(pieces, out):
    total = pieces[0]
    for k in range(1, 8):
        total = total + pieces[k]
    total = total.astype(BF16)
    for n in range(4):
        for k in range(6):
            out[6 * n + k] = total[n]


def last_kernel(pieces, first, second):
    for c, out in enumerate((first, second)):
        for sb, rows in enumerate((14, 13)):
            parts = [pieces[zh * 12 + c * 6 + sa * 2 + sb].astype(F32) for zh in range(2) for sa in range(3)]
            total = parts[0]
            for part in parts[1:]:
                total = total + part
            out[14 * sb : 14 * sb + rows] = total[0:rows]


VMEM = pl.BlockSpec(memory_space=pltpu.VMEM)
SMEM = pl.BlockSpec(memory_space=pltpu.SMEM)
HBM = pl.BlockSpec(memory_space=pltpu.HBM)


def kernel_call(body, ins, outs, scratch, flops, room=50):
    return pl.pallas_call(
        body,
        out_shape=outs,
        in_specs=ins,
        out_specs=[VMEM] * len(outs),
        scratch_shapes=scratch,
        compiler_params=pltpu.CompilerParams(vmem_limit_bytes=room * 1024 * 1024),
        cost_estimate=pl.CostEstimate(flops=flops, bytes_accessed=4_000_000, transcendentals=0),
    )


def in_hbm(*arrays):
    return [pltpu.with_memory_space_constraint(a, pltpu.HBM) for a in arrays]


def shape(*dims, dtype=BF16):
    return jax.ShapeDtypeStruct(dims, dtype)


def folded(pieces):
    return pieces.astype(F32).sum(axis=0)


def on_device(features, cotangent, blocks, w_first, w_second):
    outer, inner = kernel_call(
        halo_kernel,
        [HBM] * 3,
        [shape(1, 7, 32, C), shape(7, 64, C)],
        [pltpu.SMEM((1, SLOTS), jnp.int32), pltpu.SemaphoreType.DMA((5,))],
        1,
        40,
    )(*in_hbm(blocks, features, cotangent))
    odd = range(1, 127, 2)
    partner = lax.ppermute(inner, "c", [(0, 1), (1, 0)])
    far = lax.ppermute(outer, TILE, [(t + 2, t) for t in range(0, 126, 2)] + [(t, t + 2) for t in range(1, 126, 2)])
    near = lax.ppermute(outer, TILE, [(t, t + 1) for t in odd] + [(t + 1, t) for t in odd])
    w_first, w_second, field_z, upstream_pad, act_part, grad_part = kernel_call(
        chip_kernel,
        [VMEM, VMEM, HBM, HBM],
        [
            shape(27, C, C),
            shape(27, C, C),
            shape(3, 8, 10, 16, C),
            shape(12, 10, 16, C),
            shape(10, 128, C, dtype=F32),
            shape(10, 128, C, dtype=F32),
        ],
        [pltpu.VMEM((3, 8, 10, 16, C), BF16), pltpu.SemaphoreType.DMA((6,))],
        2_000_000_000,
        40,
    )(inner, partner, *in_hbm(w_first, w_second))
    terms, hidden, first_grad = kernel_call(
        main_kernel,
        [VMEM] * 10,
        [shape(4, 2, 14, 32, C), shape(10, 8, 16, C), shape(10, 8, 16, C)],
        [
            pltpu.VMEM((3, 4, 10, 16, C), BF16),
            pltpu.VMEM((3, 4, 10, 16, C), BF16),
            pltpu.VMEM((3, 10, 8, 16, C), BF16),
            pltpu.VMEM((12, 10, 16, C), BF16),
        ],
        2_000_000_000,
        40,
    )(inner, partner, far, near, w_first, w_second, field_z, upstream_pad, act_part, grad_part)
    block_out, input_grad = kernel_call(
        output_kernel,
        [SMEM] + [VMEM] * 6,
        [shape(1, SLOTS, 64, C)] * 2,
        [pltpu.VMEM((3, 6, 10, 16, C), BF16), pltpu.VMEM((3, 6, 10, 16, C), BF16)],
        1_400_000_000,
    )(blocks, features, cotangent, hidden, first_grad, w_first, w_second)
    terms = terms.reshape(8, 14, 32, C)
    along_x = folded(lax.all_to_all(terms, ("x", "sb"), 0, 0, tiled=True)).reshape(14, 8, 4, C)
    along_y = lax.all_to_all(along_x.transpose(1, 2, 0, 3), "y", 0, 0, tiled=True)
    copies = kernel_call(repeat_kernel, [VMEM], [shape(24, 14, C)], [], 1, 40)(along_y)[0]
    pieces = lax.all_to_all(copies, ("zh", "c", "sa", "sb"), 0, 0, tiled=True)
    first_total, second_total = kernel_call(last_kernel, [VMEM], [shape(27, C, dtype=F32)] * 2, [], 1, 40)(pieces)
    return block_out, input_grad, first_total, second_total


def solution(mesh):
    split = Mesh(mesh.devices.reshape(2, 8, 4, 2, 3, 2), TILE + SCENE)
    return jax.shard_map(
        on_device,
        mesh=split,
        in_specs=(
            P(SCENE, TILE, None, None),
            P(SCENE, TILE, None, None),
            P(SCENE, TILE),
            P(),
            P(),
        ),
        out_specs=(
            P(SCENE, TILE, None, None),
            P(SCENE, TILE, None, None),
            P(None, TILE),
            P(None, TILE),
        ),
        check_vma=False,
    )
```

```python
import jax
import jax.numpy as jnp
from jax import lax
from jax.experimental import pallas as pl
from jax.experimental.pallas import tpu as pltpu
from jax.sharding import Mesh, PartitionSpec as P

BY = 2
BZ = 4
C = 128
SLOTS = 3
TILE = ("zh", "ya", "yb", "x", "c")
SCENE = ("sa", "sb")
F32 = jnp.float32
BF16 = jnp.bfloat16


def fetch(pairs, sems, first=0):
    copies = [pltpu.make_async_copy(src, dst, sems.at[first + k]) for k, (src, dst) in enumerate(pairs)]
    for copy in copies:
        copy.start()
    return copies


def halo_kernel(blocks, features, cotangent, outer, inner, ids, sems):
    core = lax.axis_index("c")
    edge = pl.ds(pl.multiple_of(32 * core, 32), 32)
    copies = fetch(
        [
            (blocks, ids),
            (features.at[0, :, edge, :], outer.at[0, 0:3]),
            (cotangent.at[0, :, edge, :], outer.at[0, 3:6]),
            (features.at[0], inner.at[0:3]),
            (cotangent.at[0], inner.at[3:6]),
        ],
        sems,
    )
    copies[0].wait()
    row = lax.broadcasted_iota(jnp.int32, (32, C), 0)
    marks = jnp.zeros((32, C), F32)
    for j in range(SLOTS):
        marks = jnp.where(row == j, (ids[0, j] + 1).astype(F32), marks)
    outer[0, 6] = marks.astype(BF16)
    inner[6, 0:32] = marks.astype(BF16)
    inner[6, 32:64] = jnp.zeros((32, C), BF16)
    for copy in copies[1:]:
        copy.wait()


def block_masks(ids):
    upper = lax.broadcasted_iota(jnp.int32, (8, C), 0) // 4
    return [
        [[ids[j] == (upper + (4 * by + 2 * h)) for h in range(2)] for by in range(BY)]
        for j in range(SLOTS)
    ]


def live_tiles(masks):
    rows = []
    for by in range(BY):
        halves = []
        for h in range(2):
            any_slot = masks[0][by][h] | masks[1][by][h] | masks[2][by][h]
            halves.append(jnp.where(any_slot, 1.0, 0.0))
        tile = jnp.concatenate(halves, axis=0)
        rows.append(jnp.broadcast_to(tile[None], (4, 16, C)))
    return jnp.concatenate(rows, axis=0)


def to_slab(rows, masks, layers):
    count = SLOTS * layers * 16
    low = lax.broadcasted_iota(jnp.int32, (count, C), 0) % 8 < 4
    even = jnp.where(low, rows, pltpu.roll(rows, 4, 0))
    odd = jnp.where(low, pltpu.roll(rows, count - 4, 0), rows)
    shape = (SLOTS, layers, 2, 8, C)
    even, odd = even.reshape(shape), odd.reshape(shape)
    whole = []
    for by in range(BY):
        halves = []
        for h in range(2):
            pair = []
            for part in (even, odd):
                picked = jnp.zeros((layers, 2, 8, C), F32)
                for j in range(SLOTS):
                    picked = jnp.where(masks[j][by][h][None, None], part[j], picked)
                pair.append(picked)
            halves.append(jnp.stack(pair, axis=2).reshape(layers, 4, 8, C))
        whole.append(jnp.concatenate(halves, axis=2))
    return jnp.concatenate(whole, axis=1)


def from_slab(slab, masks, layers):
    low = lax.broadcasted_iota(jnp.int32, (8, C), 0) < 4
    slots = []
    for j in range(SLOTS):
        picked = jnp.zeros((layers, 4, 8, C), F32)
        for by in range(BY):
            for h in range(2):
                part = slab[:, 4 * by : 4 * by + 4, 8 * h : 8 * h + 8, :]
                picked = picked + jnp.where(masks[j][by][h][None, None], part, 0.0)
        flat = picked.reshape(layers * 32, C)
        both = (flat + pltpu.roll(flat, 4, 0)).reshape(layers, 2, 2, 8, C)
        rest = (flat + pltpu.roll(flat, layers * 32 - 4, 0)).reshape(layers, 2, 2, 8, C)
        full_even = rest[:, :, 0]
        full_odd = both[:, :, 1]
        slots.append(jnp.where(low[None, None], full_even, full_odd).reshape(layers * 16, C))
    return jnp.stack(slots)


def shifted_rows(slab, layers):
    flat = slab.reshape(layers * 128, C)
    z = lax.broadcasted_iota(jnp.int32, (layers * 128, C), 0) % 16
    before = jnp.where(z == 0, 0.0, pltpu.roll(flat, 1, 0))
    after = jnp.where(z == 15, 0.0, pltpu.roll(flat, layers * 128 - 1, 0))
    return before, flat, after


def store_shifted(out, slab, layers):
    for c, rows in enumerate(shifted_rows(slab, layers)):
        out[c, :, 1:9] = rows.astype(BF16).reshape(layers, 8, 16, C)
        out[c, :, 0] = jnp.zeros((layers, 16, C), BF16)
        out[c, :, 9] = jnp.zeros((layers, 16, C), BF16)


def patches(shifted, first, layers, back):
    rows = pl.ds(first, layers)
    return [
        (shifted[2 - c, rows, 2 - b : 10 - b] if back else shifted[c, rows, b : b + 8]).reshape(layers * 128, C)
        for b in range(3)
        for c in range(3)
    ]


def matrices(weights, k, back):
    return [weights[9 * (2 - k if back else k) + j] for j in range(9)]


def product(pieces, columns, layers, back):
    lhs = jnp.concatenate(pieces, axis=1)
    rhs = jnp.concatenate([jnp.concatenate(col, axis=1 if back else 0) for col in columns], axis=0 if back else 1)
    out = lax.dot_general(lhs, rhs, (((1,), (1 if back else 0,)), ((), ())), preferred_element_type=F32)
    out = out.reshape(layers, 128, len(columns) * C)
    return [out[:, :, n * C : (n + 1) * C] for n in range(len(columns))]


def taps(shifted, weights, layers, back=False):
    pieces = patches(shifted, 0, layers, back)
    after, same = product(pieces, [matrices(weights, 0, back), matrices(weights, 1, back)], layers, back)
    last = matrices(weights, 2, back)
    none = jnp.zeros((C, C), BF16)
    before, aside = product(pieces[:6], [last[:6], [none] * 3 + last[6:]], layers, back)
    aside = aside.reshape(layers, 8, 16, C)
    edge = jnp.zeros((layers, 1, 16, C), F32)
    moved = [edge, aside[:, :7]] if back else [aside[:, 1:], edge]
    return after, same, before + jnp.concatenate(moved, axis=1).reshape(layers, 128, C)


def inside(out, layers):
    after, same, before = out
    n = layers - 2
    return after[0:n] + same[1 : n + 1] + before[2 : n + 2]


def spread(out):
    after, same, before = out
    none = jnp.zeros((1, 128, C), F32)
    return (
        jnp.concatenate([none, none, after], axis=0)
        + jnp.concatenate([none, same, none], axis=0)
        + jnp.concatenate([before, none, none], axis=0)
    )


def completed(part, shifted, weights, back=False):
    after, left = product(
        patches(shifted, 0, 2, back), [matrices(weights, 0, back), matrices(weights, 1, back)], 2, back
    )
    right, before = product(
        patches(shifted, 2, 2, back), [matrices(weights, 1, back), matrices(weights, 2, back)], 2, back
    )
    return jnp.concatenate(
        [
            part[0:1] + after[0:1] + left[1:2],
            part[1:2] + after[1:2],
            part[2:8],
            part[8:9] + before[0:1],
            part[9:10] + right[0:1] + before[1:2],
        ],
        axis=0,
    )


def weight_terms(order, shifted_layers, padded, terms):
    turned = jnp.concatenate(
        [
            lax.dot_general(order, rows, (((1,), (1,)), ((), ())), preferred_element_type=F32).astype(BF16)
            for rows in shifted_layers
        ],
        axis=0,
    )
    rhs = jnp.concatenate([padded(a, b) for a in range(3) for b in range(3)], axis=1)
    out = jnp.dot(turned, rhs, preferred_element_type=F32)
    for a in range(3):
        for b in range(3):
            for c in range(3):
                piece = out[c * C : (c + 1) * C, (3 * a + b) * C : (3 * a + b + 1) * C]
                half, tap = divmod(9 * a + 3 * b + c, 14)
                terms[:, half, tap] = piece.astype(BF16).reshape(8, 16, C)
    terms[:, 1, 13] = jnp.zeros((8, 16, C), BF16)


def pad_store(out, slab):
    out[0:2] = jnp.zeros((2, 10, 16, C), BF16)
    out[10:12] = jnp.zeros((2, 10, 16, C), BF16)
    out[2:10, 0] = jnp.zeros((8, 16, C), BF16)
    out[2:10, 9] = jnp.zeros((8, 16, C), BF16)
    out[2:10, 1:9] = slab.astype(BF16)


def ids_of(tile):
    rows = tile.astype(F32).astype(jnp.int32)
    return [jnp.broadcast_to(rows[j : j + 1] - 1, (8, C)) for j in range(SLOTS)]


def choose(even, one, other):
    return [jnp.where(even, p, q) for p, q in zip(one, other)]


def chip_ids(own, partner, even):
    own, partner = ids_of(own[6, 0:16]), ids_of(partner[6, 0:16])
    return choose(even, own, partner), choose(even, partner, own)


def chip_kernel(
    own, partner, w_first_hbm, w_second_hbm,
    w_first, w_second, field_z, upstream_pad, act_part, grad_part,
    upstream_z, sems,
):
    thirds = [pl.ds(9 * k, 9) for k in range(3)]
    one = fetch([(w_first_hbm.at[k], w_first.at[k]) for k in thirds], sems, 0)
    even = lax.axis_index("c") == 0
    masks = [block_masks(ids) for ids in chip_ids(own, partner, even)]

    def field(which):
        partner_rows = partner[3 * which : 3 * which + 3].astype(F32).reshape(192, C)
        own_rows = own[3 * which : 3 * which + 3].astype(F32).reshape(192, C)
        parts = (
            to_slab(jnp.where(even, own_rows, partner_rows), masks[0], 4),
            to_slab(jnp.where(even, partner_rows, own_rows), masks[1], 4),
        )
        return jnp.concatenate(parts, axis=0)

    store_shifted(field_z, field(0), 8)
    two = fetch([(w_second_hbm.at[k], w_second.at[k]) for k in thirds], sems, 3)
    upstream = field(1)
    store_shifted(upstream_z, upstream, 8)
    pad_store(upstream_pad, upstream)
    for copy in one:
        copy.wait()
    act_part[...] = spread(taps(field_z, w_first, 8))
    for copy in two:
        copy.wait()
    grad_part[...] = spread(taps(upstream_z, w_second, 8, True))


def main_kernel(
    own, partner, far, near, w_first, w_second, field_z, upstream_pad, act_part, grad_part,
    terms, hidden_out, grad_out,
    outer_z, outer_up_z, stage_z, padded,
):
    core = lax.axis_index("c")
    even = core == 0
    near_ids, far_ids = ids_of(near[0, 6, 0:16]), ids_of(far[0, 6, 0:16])
    left, right = (block_masks(ids) for ids in (choose(even, near_ids, far_ids), choose(even, far_ids, near_ids)))
    lower, upper = (block_masks(ids) for ids in chip_ids(own, partner, even))

    def field(which):
        near_rows = near[0, 3 * which : 3 * which + 3].astype(F32).reshape(96, C)
        far_rows = far[0, 3 * which : 3 * which + 3].astype(F32).reshape(96, C)
        parts = (
            to_slab(jnp.where(even, near_rows, far_rows), left, 2),
            to_slab(jnp.where(even, far_rows, near_rows), right, 2),
        )
        return jnp.concatenate(parts, axis=0)

    store_shifted(outer_z, field(0), 4)
    store_shifted(outer_up_z, field(1), 4)
    first_act = completed(act_part[...], outer_z, w_first).reshape(10, 8, 16, C)
    live = jnp.concatenate(
        [
            live_tiles(left)[None],
            jnp.broadcast_to(live_tiles(lower)[None], (4, 8, 16, C)),
            jnp.broadcast_to(live_tiles(upper)[None], (4, 8, 16, C)),
            live_tiles(right)[None],
        ],
        axis=0,
    )
    gate = 1.0 / (1.0 + jnp.exp(-first_act))
    hidden = live * (first_act * gate)
    hidden_out[...] = hidden.astype(BF16)
    slope = live * (gate * (1.0 + first_act * (1.0 - gate)))
    hidden_grad = completed(grad_part[...], outer_up_z, w_second, True).reshape(10, 8, 16, C)
    grad_out[...] = (hidden_grad * slope).astype(BF16)

    @pl.when(even)
    def _():
        for c in range(3):
            stage_z[c, 0] = outer_z[c, 1, 1:9]
            stage_z[c, 1:9] = field_z[c, :, 1:9]
            stage_z[c, 9] = outer_z[c, 2, 1:9]
        pad_store(padded, grad_out[1:9])

    @pl.when(core == 1)
    def _():
        for c, rows in enumerate(shifted_rows(hidden_out[...].astype(F32), 10)):
            stage_z[c] = rows.astype(BF16).reshape(10, 8, 16, C)
        padded[...] = upstream_pad[...]

    r = lax.broadcasted_iota(jnp.int32, (C, C), 0)
    i = lax.broadcasted_iota(jnp.int32, (C, C), 1)
    y = (r // 4) % 4 * 2 + r // 64
    wanted = (((r // 2) % 2 * 8 + y) * 4 + (r // 16) % 4) * 2 + r % 2
    order = jnp.where(i == wanted, 1.0, 0.0).astype(BF16)
    weight_terms(
        order,
        [stage_z[c].reshape(1280, C) for c in range(3)],
        lambda a, b: padded[2 - a : 12 - a, 2 - b : 10 - b].reshape(1280, C),
        terms,
    )


def output_kernel(
    blocks, features, cotangent, hidden, first_grad, w_first, w_second,
    block_out, input_grad,
    hidden_z, grad_z,
):
    mine = pl.ds(4 * lax.axis_index("c"), 6)
    own = block_masks([blocks[0, j] for j in range(SLOTS)])
    store_shifted(hidden_z, hidden[mine].astype(F32), 6)
    store_shifted(grad_z, first_grad[mine].astype(F32), 6)
    second_act = from_slab(inside(taps(hidden_z, w_second, 6), 6).reshape(4, 8, 16, C), own, 4)
    back = from_slab(inside(taps(grad_z, w_first, 6, True), 6).reshape(4, 8, 16, C), own, 4)
    for j in range(SLOTS):
        live = jnp.where(blocks[0, j] < BY * BZ, 1.0, 0.0)
        block_out[0, j] = (live * (features[0, j].astype(F32) + second_act[j])).astype(BF16)
        input_grad[0, j] = (live * (cotangent[0, j].astype(F32) + back[j])).astype(BF16)


def repeat_kernel(pieces, out):
    total = pieces[0]
    for k in range(1, 4):
        total = total + pieces[k]
    total = total.astype(BF16)
    for n in range(4):
        for k in range(6):
            out[6 * n + k] = total[n]


def last_kernel(pieces, first, second):
    for c, out in enumerate((first, second)):
        for sb, rows in enumerate((14, 13)):
            parts = [pieces[zh * 12 + c * 6 + sa * 2 + sb].astype(F32) for zh in range(2) for sa in range(3)]
            total = parts[0]
            for part in parts[1:]:
                total = total + part
            out[14 * sb : 14 * sb + rows] = total[0:rows]


VMEM = pl.BlockSpec(memory_space=pltpu.VMEM)
SMEM = pl.BlockSpec(memory_space=pltpu.SMEM)
HBM = pl.BlockSpec(memory_space=pltpu.HBM)


def kernel_call(body, ins, outs, scratch, flops, room=50):
    return pl.pallas_call(
        body,
        out_shape=outs,
        in_specs=ins,
        out_specs=[VMEM] * len(outs),
        scratch_shapes=scratch,
        compiler_params=pltpu.CompilerParams(vmem_limit_bytes=room * 1024 * 1024),
        cost_estimate=pl.CostEstimate(flops=flops, bytes_accessed=4_000_000, transcendentals=0),
    )


def in_hbm(*arrays):
    return [pltpu.with_memory_space_constraint(a, pltpu.HBM) for a in arrays]


def shape(*dims, dtype=BF16):
    return jax.ShapeDtypeStruct(dims, dtype)


def folded(pieces):
    return pieces.astype(F32).sum(axis=0)


def on_device(features, cotangent, blocks, w_first, w_second):
    outer, inner = kernel_call(
        halo_kernel,
        [HBM] * 3,
        [shape(1, 7, 32, C), shape(7, 64, C)],
        [pltpu.SMEM((1, SLOTS), jnp.int32), pltpu.SemaphoreType.DMA((5,))],
        1,
        40,
    )(*in_hbm(blocks, features, cotangent))
    odd = range(1, 127, 2)
    partner = lax.ppermute(inner, "c", [(0, 1), (1, 0)])
    far = lax.ppermute(outer, TILE, [(t + 2, t) for t in range(0, 126, 2)] + [(t, t + 2) for t in range(1, 126, 2)])
    near = lax.ppermute(outer, TILE, [(t, t + 1) for t in odd] + [(t + 1, t) for t in odd])
    w_first, w_second, field_z, upstream_pad, act_part, grad_part = kernel_call(
        chip_kernel,
        [VMEM, VMEM, HBM, HBM],
        [
            shape(27, C, C),
            shape(27, C, C),
            shape(3, 8, 10, 16, C),
            shape(12, 10, 16, C),
            shape(10, 128, C, dtype=F32),
            shape(10, 128, C, dtype=F32),
        ],
        [pltpu.VMEM((3, 8, 10, 16, C), BF16), pltpu.SemaphoreType.DMA((6,))],
        2_000_000_000,
        40,
    )(inner, partner, *in_hbm(w_first, w_second))
    terms, hidden, first_grad = kernel_call(
        main_kernel,
        [VMEM] * 10,
        [shape(8, 2, 14, 16, C), shape(10, 8, 16, C), shape(10, 8, 16, C)],
        [
            pltpu.VMEM((3, 4, 10, 16, C), BF16),
            pltpu.VMEM((3, 4, 10, 16, C), BF16),
            pltpu.VMEM((3, 10, 8, 16, C), BF16),
            pltpu.VMEM((12, 10, 16, C), BF16),
        ],
        2_000_000_000,
        40,
    )(inner, partner, far, near, w_first, w_second, field_z, upstream_pad, act_part, grad_part)
    block_out, input_grad = kernel_call(
        output_kernel,
        [SMEM] + [VMEM] * 6,
        [shape(1, SLOTS, 64, C)] * 2,
        [pltpu.VMEM((3, 6, 10, 16, C), BF16), pltpu.VMEM((3, 6, 10, 16, C), BF16)],
        1_400_000_000,
    )(blocks, features, cotangent, hidden, first_grad, w_first, w_second)
    terms = terms.reshape(16, 14, 16, C)
    along_x = folded(lax.all_to_all(terms, ("yb", "x", "sb"), 0, 0, tiled=True)).reshape(14, 4, 4, C)
    along_y = lax.all_to_all(along_x.transpose(1, 2, 0, 3), "ya", 0, 0, tiled=True)
    copies = kernel_call(repeat_kernel, [VMEM], [shape(24, 14, C)], [], 1, 40)(along_y)[0]
    pieces = lax.all_to_all(copies, ("zh", "c", "sa", "sb"), 0, 0, tiled=True)
    first_total, second_total = kernel_call(last_kernel, [VMEM], [shape(27, C, dtype=F32)] * 2, [], 1, 40)(pieces)
    return block_out, input_grad, first_total, second_total


def solution(mesh):
    split = Mesh(mesh.devices.reshape(2, 4, 2, 4, 2, 3, 2), TILE + SCENE)
    return jax.shard_map(
        on_device,
        mesh=split,
        in_specs=(
            P(SCENE, TILE, None, None),
            P(SCENE, TILE, None, None),
            P(SCENE, TILE),
            P(),
            P(),
        ),
        out_specs=(
            P(SCENE, TILE, None, None),
            P(SCENE, TILE, None, None),
            P(None, TILE),
            P(None, TILE),
        ),
        check_vma=False,
    )
```

```python
import jax
import jax.numpy as jnp
from jax import lax
from jax.experimental import pallas as pl
from jax.experimental.pallas import tpu as pltpu
from jax.sharding import Mesh, PartitionSpec as P

BY = 2
BZ = 4
C = 128
SLOTS = 3
TILE = ("zh", "ya", "yb", "x", "c")
SCENE = ("sa", "sb")
F32 = jnp.float32
BF16 = jnp.bfloat16


def fetch(pairs, sems, first=0):
    copies = [pltpu.make_async_copy(src, dst, sems.at[first + k]) for k, (src, dst) in enumerate(pairs)]
    for copy in copies:
        copy.start()
    return copies


def halo_kernel(blocks, features, cotangent, outer, inner, ids, sems):
    core = lax.axis_index("c")
    edge = pl.ds(pl.multiple_of(32 * core, 32), 32)
    copies = fetch(
        [
            (blocks, ids),
            (features.at[0, :, edge, :], outer.at[0, 0:3]),
            (cotangent.at[0, :, edge, :], outer.at[0, 3:6]),
            (features.at[0], inner.at[0:3]),
            (cotangent.at[0], inner.at[3:6]),
        ],
        sems,
    )
    copies[0].wait()
    row = lax.broadcasted_iota(jnp.int32, (32, C), 0)
    marks = jnp.zeros((32, C), F32)
    for j in range(SLOTS):
        marks = jnp.where(row == j, (ids[0, j] + 1).astype(F32), marks)
    outer[0, 6] = marks.astype(BF16)
    inner[6, 0:32] = marks.astype(BF16)
    inner[6, 32:64] = jnp.zeros((32, C), BF16)
    for copy in copies[1:]:
        copy.wait()


def block_masks(ids):
    upper = lax.broadcasted_iota(jnp.int32, (8, C), 0) // 4
    return [
        [[ids[j] == (upper + (4 * by + 2 * h)) for h in range(2)] for by in range(BY)]
        for j in range(SLOTS)
    ]


def live_tiles(masks):
    rows = []
    for by in range(BY):
        halves = []
        for h in range(2):
            any_slot = masks[0][by][h] | masks[1][by][h] | masks[2][by][h]
            halves.append(jnp.where(any_slot, 1.0, 0.0))
        tile = jnp.concatenate(halves, axis=0)
        rows.append(jnp.broadcast_to(tile[None], (4, 16, C)))
    return jnp.concatenate(rows, axis=0)


def to_slab(rows, masks, layers):
    count = SLOTS * layers * 16
    low = lax.broadcasted_iota(jnp.int32, (count, C), 0) % 8 < 4
    even = jnp.where(low, rows, pltpu.roll(rows, 4, 0))
    odd = jnp.where(low, pltpu.roll(rows, count - 4, 0), rows)
    shape = (SLOTS, layers, 2, 8, C)
    even, odd = even.reshape(shape), odd.reshape(shape)
    whole = []
    for by in range(BY):
        halves = []
        for h in range(2):
            pair = []
            for part in (even, odd):
                picked = jnp.zeros((layers, 2, 8, C), F32)
                for j in range(SLOTS):
                    picked = jnp.where(masks[j][by][h][None, None], part[j], picked)
                pair.append(picked)
            halves.append(jnp.stack(pair, axis=2).reshape(layers, 4, 8, C))
        whole.append(jnp.concatenate(halves, axis=2))
    return jnp.concatenate(whole, axis=1)


def from_slab(slab, masks, layers):
    low = lax.broadcasted_iota(jnp.int32, (8, C), 0) < 4
    slots = []
    for j in range(SLOTS):
        picked = jnp.zeros((layers, 4, 8, C), F32)
        for by in range(BY):
            for h in range(2):
                part = slab[:, 4 * by : 4 * by + 4, 8 * h : 8 * h + 8, :]
                picked = picked + jnp.where(masks[j][by][h][None, None], part, 0.0)
        flat = picked.reshape(layers * 32, C)
        both = (flat + pltpu.roll(flat, 4, 0)).reshape(layers, 2, 2, 8, C)
        rest = (flat + pltpu.roll(flat, layers * 32 - 4, 0)).reshape(layers, 2, 2, 8, C)
        full_even = rest[:, :, 0]
        full_odd = both[:, :, 1]
        slots.append(jnp.where(low[None, None], full_even, full_odd).reshape(layers * 16, C))
    return jnp.stack(slots)


def shifted_rows(slab, layers):
    flat = slab.reshape(layers * 128, C)
    z = lax.broadcasted_iota(jnp.int32, (layers * 128, C), 0) % 16
    before = jnp.where(z == 0, 0.0, pltpu.roll(flat, 1, 0))
    after = jnp.where(z == 15, 0.0, pltpu.roll(flat, layers * 128 - 1, 0))
    return before, flat, after


def store_shifted(out, slab, layers):
    for c, rows in enumerate(shifted_rows(slab, layers)):
        out[c, :, 1:9] = rows.astype(BF16).reshape(layers, 8, 16, C)
        out[c, :, 0] = jnp.zeros((layers, 16, C), BF16)
        out[c, :, 9] = jnp.zeros((layers, 16, C), BF16)


def patches(shifted, first, layers, back):
    rows = pl.ds(first, layers)
    return [
        (shifted[2 - c, rows, 2 - b : 10 - b] if back else shifted[c, rows, b : b + 8]).reshape(layers * 128, C)
        for b in range(3)
        for c in range(3)
    ]


def matrices(weights, k, back):
    return [weights[9 * (2 - k if back else k) + j] for j in range(9)]


def product(pieces, columns, layers, back):
    lhs = jnp.concatenate(pieces, axis=1)
    rhs = jnp.concatenate([jnp.concatenate(col, axis=1 if back else 0) for col in columns], axis=0 if back else 1)
    out = lax.dot_general(lhs, rhs, (((1,), (1 if back else 0,)), ((), ())), preferred_element_type=F32)
    out = out.reshape(layers, 128, len(columns) * C)
    return [out[:, :, n * C : (n + 1) * C] for n in range(len(columns))]


def taps(shifted, weights, layers, back=False):
    pieces = patches(shifted, 0, layers, back)
    after, same = product(pieces, [matrices(weights, 0, back), matrices(weights, 1, back)], layers, back)
    last = matrices(weights, 2, back)
    none = jnp.zeros((C, C), BF16)
    before, aside = product(pieces[:6], [last[:6], [none] * 3 + last[6:]], layers, back)
    aside = aside.reshape(layers, 8, 16, C)
    edge = jnp.zeros((layers, 1, 16, C), F32)
    moved = [edge, aside[:, :7]] if back else [aside[:, 1:], edge]
    return after, same, before + jnp.concatenate(moved, axis=1).reshape(layers, 128, C)


def inside(out, layers):
    after, same, before = out
    n = layers - 2
    return after[0:n] + same[1 : n + 1] + before[2 : n + 2]


def spread(out):
    after, same, before = out
    none = jnp.zeros((1, 128, C), F32)
    return (
        jnp.concatenate([none, none, after], axis=0)
        + jnp.concatenate([none, same, none], axis=0)
        + jnp.concatenate([before, none, none], axis=0)
    )


def completed(part, shifted, weights, back=False):
    after, left = product(
        patches(shifted, 0, 2, back), [matrices(weights, 0, back), matrices(weights, 1, back)], 2, back
    )
    right, before = product(
        patches(shifted, 2, 2, back), [matrices(weights, 1, back), matrices(weights, 2, back)], 2, back
    )
    return jnp.concatenate(
        [
            part[0:1] + after[0:1] + left[1:2],
            part[1:2] + after[1:2],
            part[2:8],
            part[8:9] + before[0:1],
            part[9:10] + right[0:1] + before[1:2],
        ],
        axis=0,
    )


def weight_terms(order, shifted_layers, padded, terms):
    turned = jnp.concatenate(
        [
            lax.dot_general(order, rows, (((1,), (1,)), ((), ())), preferred_element_type=F32).astype(BF16)
            for rows in shifted_layers
        ],
        axis=0,
    )
    rhs = jnp.concatenate([padded(a, b) for a in range(3) for b in range(3)], axis=1)
    out = jnp.dot(turned, rhs, preferred_element_type=F32)
    for a in range(3):
        for b in range(3):
            for c in range(3):
                piece = out[c * C : (c + 1) * C, (3 * a + b) * C : (3 * a + b + 1) * C]
                half, tap = divmod(9 * a + 3 * b + c, 14)
                terms[:, half, tap] = piece.astype(BF16).reshape(8, 16, C)
    terms[:, 1, 13] = jnp.zeros((8, 16, C), BF16)


def pad_store(out, slab):
    out[0:2] = jnp.zeros((2, 10, 16, C), BF16)
    out[10:12] = jnp.zeros((2, 10, 16, C), BF16)
    out[2:10, 0] = jnp.zeros((8, 16, C), BF16)
    out[2:10, 9] = jnp.zeros((8, 16, C), BF16)
    out[2:10, 1:9] = slab.astype(BF16)


def ids_of(tile):
    rows = tile.astype(F32).astype(jnp.int32)
    return [jnp.broadcast_to(rows[j : j + 1] - 1, (8, C)) for j in range(SLOTS)]


def choose(even, one, other):
    return [jnp.where(even, p, q) for p, q in zip(one, other)]


def chip_ids(own, partner, even):
    own, partner = ids_of(own[6, 0:16]), ids_of(partner[6, 0:16])
    return choose(even, own, partner), choose(even, partner, own)


def chip_kernel(
    own, partner, w_first_hbm, w_second_hbm,
    w_first, w_second, field_z, upstream_pad, act_part, grad_part,
    upstream_z, sems,
):
    thirds = [pl.ds(9 * k, 9) for k in range(3)]
    one = fetch([(w_first_hbm.at[k], w_first.at[k]) for k in thirds], sems, 0)
    even = lax.axis_index("c") == 0
    masks = [block_masks(ids) for ids in chip_ids(own, partner, even)]

    def field(which):
        partner_rows = partner[3 * which : 3 * which + 3].astype(F32).reshape(192, C)
        own_rows = own[3 * which : 3 * which + 3].astype(F32).reshape(192, C)
        parts = (
            to_slab(jnp.where(even, own_rows, partner_rows), masks[0], 4),
            to_slab(jnp.where(even, partner_rows, own_rows), masks[1], 4),
        )
        return jnp.concatenate(parts, axis=0)

    two = fetch([(w_second_hbm.at[k], w_second.at[k]) for k in thirds], sems, 3)
    store_shifted(field_z, field(0), 8)
    upstream = field(1)
    store_shifted(upstream_z, upstream, 8)
    pad_store(upstream_pad, upstream)
    for copy in one:
        copy.wait()
    for copy in two:
        copy.wait()
    act_part[...] = spread(taps(field_z, w_first, 8))
    grad_part[...] = spread(taps(upstream_z, w_second, 8, True))


def main_kernel(
    own, partner, far, near, w_first, w_second, field_z, upstream_pad, act_part, grad_part,
    terms, hidden_out, grad_out,
    outer_z, outer_up_z, stage_z, padded,
):
    core = lax.axis_index("c")
    even = core == 0
    near_ids, far_ids = ids_of(near[0, 6, 0:16]), ids_of(far[0, 6, 0:16])
    left, right = (block_masks(ids) for ids in (choose(even, near_ids, far_ids), choose(even, far_ids, near_ids)))
    lower, upper = (block_masks(ids) for ids in chip_ids(own, partner, even))

    def field(which):
        near_rows = near[0, 3 * which : 3 * which + 3].astype(F32).reshape(96, C)
        far_rows = far[0, 3 * which : 3 * which + 3].astype(F32).reshape(96, C)
        parts = (
            to_slab(jnp.where(even, near_rows, far_rows), left, 2),
            to_slab(jnp.where(even, far_rows, near_rows), right, 2),
        )
        return jnp.concatenate(parts, axis=0)

    store_shifted(outer_z, field(0), 4)
    store_shifted(outer_up_z, field(1), 4)
    first_act = completed(act_part[...], outer_z, w_first).reshape(10, 8, 16, C)
    live = jnp.concatenate(
        [
            live_tiles(left)[None],
            jnp.broadcast_to(live_tiles(lower)[None], (4, 8, 16, C)),
            jnp.broadcast_to(live_tiles(upper)[None], (4, 8, 16, C)),
            live_tiles(right)[None],
        ],
        axis=0,
    )
    gate = 1.0 / (1.0 + jnp.exp(-first_act))
    hidden = live * (first_act * gate)
    hidden_out[...] = hidden.astype(BF16)
    slope = live * (gate * (1.0 + first_act * (1.0 - gate)))
    hidden_grad = completed(grad_part[...], outer_up_z, w_second, True).reshape(10, 8, 16, C)
    grad_out[...] = (hidden_grad * slope).astype(BF16)

    @pl.when(even)
    def _():
        for c in range(3):
            stage_z[c, 0] = outer_z[c, 1, 1:9]
            stage_z[c, 1:9] = field_z[c, :, 1:9]
            stage_z[c, 9] = outer_z[c, 2, 1:9]
        pad_store(padded, grad_out[1:9])

    @pl.when(core == 1)
    def _():
        for c, rows in enumerate(shifted_rows(hidden_out[...].astype(F32), 10)):
            stage_z[c] = rows.astype(BF16).reshape(10, 8, 16, C)
        padded[...] = upstream_pad[...]

    r = lax.broadcasted_iota(jnp.int32, (C, C), 0)
    i = lax.broadcasted_iota(jnp.int32, (C, C), 1)
    y = (r // 4) % 4 * 2 + r // 64
    wanted = (((r // 2) % 2 * 8 + y) * 4 + (r // 16) % 4) * 2 + r % 2
    order = jnp.where(i == wanted, 1.0, 0.0).astype(BF16)
    weight_terms(
        order,
        [stage_z[c].reshape(1280, C) for c in range(3)],
        lambda a, b: padded[2 - a : 12 - a, 2 - b : 10 - b].reshape(1280, C),
        terms,
    )


def output_kernel(
    blocks, features, cotangent, hidden, first_grad, w_first, w_second,
    block_out, input_grad,
    hidden_z, grad_z,
):
    mine = pl.ds(4 * lax.axis_index("c"), 6)
    own = block_masks([blocks[0, j] for j in range(SLOTS)])
    store_shifted(hidden_z, hidden[mine].astype(F32), 6)
    store_shifted(grad_z, first_grad[mine].astype(F32), 6)
    second_act = from_slab(inside(taps(hidden_z, w_second, 6), 6).reshape(4, 8, 16, C), own, 4)
    back = from_slab(inside(taps(grad_z, w_first, 6, True), 6).reshape(4, 8, 16, C), own, 4)
    for j in range(SLOTS):
        live = jnp.where(blocks[0, j] < BY * BZ, 1.0, 0.0)
        block_out[0, j] = (live * (features[0, j].astype(F32) + second_act[j])).astype(BF16)
        input_grad[0, j] = (live * (cotangent[0, j].astype(F32) + back[j])).astype(BF16)


def repeat_kernel(pieces, out):
    total = pieces[0]
    for k in range(1, 4):
        total = total + pieces[k]
    total = total.astype(BF16)
    for n in range(4):
        for k in range(6):
            out[6 * n + k] = total[n]


def last_kernel(pieces, first, second):
    for c, out in enumerate((first, second)):
        for sb, rows in enumerate((14, 13)):
            parts = [pieces[zh * 12 + c * 6 + sa * 2 + sb].astype(F32) for zh in range(2) for sa in range(3)]
            total = parts[0]
            for part in parts[1:]:
                total = total + part
            out[14 * sb : 14 * sb + rows] = total[0:rows]


VMEM = pl.BlockSpec(memory_space=pltpu.VMEM)
SMEM = pl.BlockSpec(memory_space=pltpu.SMEM)
HBM = pl.BlockSpec(memory_space=pltpu.HBM)


def kernel_call(body, ins, outs, scratch, flops, room=50):
    return pl.pallas_call(
        body,
        out_shape=outs,
        in_specs=ins,
        out_specs=[VMEM] * len(outs),
        scratch_shapes=scratch,
        compiler_params=pltpu.CompilerParams(vmem_limit_bytes=room * 1024 * 1024),
        cost_estimate=pl.CostEstimate(flops=flops, bytes_accessed=4_000_000, transcendentals=0),
    )


def in_hbm(*arrays):
    return [pltpu.with_memory_space_constraint(a, pltpu.HBM) for a in arrays]


def shape(*dims, dtype=BF16):
    return jax.ShapeDtypeStruct(dims, dtype)


def folded(pieces):
    return pieces.astype(F32).sum(axis=0)


def on_device(features, cotangent, blocks, w_first, w_second):
    outer, inner = kernel_call(
        halo_kernel,
        [HBM] * 3,
        [shape(1, 7, 32, C), shape(7, 64, C)],
        [pltpu.SMEM((1, SLOTS), jnp.int32), pltpu.SemaphoreType.DMA((5,))],
        1,
        40,
    )(*in_hbm(blocks, features, cotangent))
    odd = range(1, 127, 2)
    partner = lax.ppermute(inner, "c", [(0, 1), (1, 0)])
    far = lax.ppermute(outer, TILE, [(t + 2, t) for t in range(0, 126, 2)] + [(t, t + 2) for t in range(1, 126, 2)])
    near = lax.ppermute(outer, TILE, [(t, t + 1) for t in odd] + [(t + 1, t) for t in odd])
    w_first, w_second, field_z, upstream_pad, act_part, grad_part = kernel_call(
        chip_kernel,
        [VMEM, VMEM, HBM, HBM],
        [
            shape(27, C, C),
            shape(27, C, C),
            shape(3, 8, 10, 16, C),
            shape(12, 10, 16, C),
            shape(10, 128, C, dtype=F32),
            shape(10, 128, C, dtype=F32),
        ],
        [pltpu.VMEM((3, 8, 10, 16, C), BF16), pltpu.SemaphoreType.DMA((6,))],
        2_000_000_000,
        40,
    )(inner, partner, *in_hbm(w_first, w_second))
    terms, hidden, first_grad = kernel_call(
        main_kernel,
        [VMEM] * 10,
        [shape(8, 2, 14, 16, C), shape(10, 8, 16, C), shape(10, 8, 16, C)],
        [
            pltpu.VMEM((3, 4, 10, 16, C), BF16),
            pltpu.VMEM((3, 4, 10, 16, C), BF16),
            pltpu.VMEM((3, 10, 8, 16, C), BF16),
            pltpu.VMEM((12, 10, 16, C), BF16),
        ],
        2_000_000_000,
        40,
    )(inner, partner, far, near, w_first, w_second, field_z, upstream_pad, act_part, grad_part)
    block_out, input_grad = kernel_call(
        output_kernel,
        [SMEM] + [VMEM] * 6,
        [shape(1, SLOTS, 64, C)] * 2,
        [pltpu.VMEM((3, 6, 10, 16, C), BF16), pltpu.VMEM((3, 6, 10, 16, C), BF16)],
        1_400_000_000,
    )(blocks, features, cotangent, hidden, first_grad, w_first, w_second)
    terms = terms.reshape(16, 14, 16, C)
    along_x = folded(lax.all_to_all(terms, ("yb", "x", "sb"), 0, 0, tiled=True)).reshape(14, 4, 4, C)
    along_y = lax.all_to_all(along_x.transpose(1, 2, 0, 3), "ya", 0, 0, tiled=True)
    copies = kernel_call(repeat_kernel, [VMEM], [shape(24, 14, C)], [], 1, 40)(along_y)[0]
    pieces = lax.all_to_all(copies, ("zh", "c", "sa", "sb"), 0, 0, tiled=True)
    first_total, second_total = kernel_call(last_kernel, [VMEM], [shape(27, C, dtype=F32)] * 2, [], 1, 40)(pieces)
    return block_out, input_grad, first_total, second_total


def solution(mesh):
    split = Mesh(mesh.devices.reshape(2, 4, 2, 4, 2, 3, 2), TILE + SCENE)
    return jax.shard_map(
        on_device,
        mesh=split,
        in_specs=(
            P(SCENE, TILE, None, None),
            P(SCENE, TILE, None, None),
            P(SCENE, TILE),
            P(),
            P(),
        ),
        out_specs=(
            P(SCENE, TILE, None, None),
            P(SCENE, TILE, None, None),
            P(None, TILE),
            P(None, TILE),
        ),
        check_vma=False,
    )
```

```python
import jax
import jax.numpy as jnp
from jax import lax
from jax.experimental import pallas as pl
from jax.experimental.pallas import tpu as pltpu
from jax.sharding import Mesh, PartitionSpec as P

BY = 2
BZ = 4
C = 128
SLOTS = 3
TILE = ("zh", "ya", "yb", "x", "c")
SCENE = ("sa", "sb")
F32 = jnp.float32
BF16 = jnp.bfloat16


def fetch(pairs, sems, first=0):
    copies = [pltpu.make_async_copy(src, dst, sems.at[first + k]) for k, (src, dst) in enumerate(pairs)]
    for copy in copies:
        copy.start()
    return copies


def halo_kernel(blocks, features, cotangent, outer, inner, ids, sems):
    core = lax.axis_index("c")
    edge = pl.ds(pl.multiple_of(32 * core, 32), 32)
    copies = fetch(
        [
            (blocks, ids),
            (features.at[0, :, edge, :], outer.at[0, 0:3]),
            (cotangent.at[0, :, edge, :], outer.at[0, 3:6]),
            (features.at[0], inner.at[0:3]),
            (cotangent.at[0], inner.at[3:6]),
        ],
        sems,
    )
    copies[0].wait()
    row = lax.broadcasted_iota(jnp.int32, (32, C), 0)
    marks = jnp.zeros((32, C), F32)
    for j in range(SLOTS):
        marks = jnp.where(row == j, (ids[0, j] + 1).astype(F32), marks)
    outer[0, 6] = marks.astype(BF16)
    inner[6, 0:32] = marks.astype(BF16)
    inner[6, 32:64] = jnp.zeros((32, C), BF16)
    for copy in copies[1:]:
        copy.wait()


def block_masks(ids):
    upper = lax.broadcasted_iota(jnp.int32, (8, C), 0) // 4
    return [
        [[ids[j] == (upper + (4 * by + 2 * h)) for h in range(2)] for by in range(BY)]
        for j in range(SLOTS)
    ]


def live_tiles(masks):
    rows = []
    for by in range(BY):
        halves = []
        for h in range(2):
            any_slot = masks[0][by][h] | masks[1][by][h] | masks[2][by][h]
            halves.append(jnp.where(any_slot, 1.0, 0.0))
        tile = jnp.concatenate(halves, axis=0)
        rows.append(jnp.broadcast_to(tile[None], (4, 16, C)))
    return jnp.concatenate(rows, axis=0)


def to_slab(rows, masks, layers):
    count = SLOTS * layers * 16
    low = lax.broadcasted_iota(jnp.int32, (count, C), 0) % 8 < 4
    even = jnp.where(low, rows, pltpu.roll(rows, 4, 0))
    odd = jnp.where(low, pltpu.roll(rows, count - 4, 0), rows)
    shape = (SLOTS, layers, 2, 8, C)
    even, odd = even.reshape(shape), odd.reshape(shape)
    whole = []
    for by in range(BY):
        halves = []
        for h in range(2):
            pair = []
            for part in (even, odd):
                picked = jnp.zeros((layers, 2, 8, C), F32)
                for j in range(SLOTS):
                    picked = jnp.where(masks[j][by][h][None, None], part[j], picked)
                pair.append(picked)
            halves.append(jnp.stack(pair, axis=2).reshape(layers, 4, 8, C))
        whole.append(jnp.concatenate(halves, axis=2))
    return jnp.concatenate(whole, axis=1)


def from_slab(slab, masks, layers):
    low = lax.broadcasted_iota(jnp.int32, (8, C), 0) < 4
    slots = []
    for j in range(SLOTS):
        picked = jnp.zeros((layers, 4, 8, C), F32)
        for by in range(BY):
            for h in range(2):
                part = slab[:, 4 * by : 4 * by + 4, 8 * h : 8 * h + 8, :]
                picked = picked + jnp.where(masks[j][by][h][None, None], part, 0.0)
        flat = picked.reshape(layers * 32, C)
        both = (flat + pltpu.roll(flat, 4, 0)).reshape(layers, 2, 2, 8, C)
        rest = (flat + pltpu.roll(flat, layers * 32 - 4, 0)).reshape(layers, 2, 2, 8, C)
        full_even = rest[:, :, 0]
        full_odd = both[:, :, 1]
        slots.append(jnp.where(low[None, None], full_even, full_odd).reshape(layers * 16, C))
    return jnp.stack(slots)


def shifted_rows(slab, layers):
    flat = slab.reshape(layers * 128, C)
    z = lax.broadcasted_iota(jnp.int32, (layers * 128, C), 0) % 16
    before = jnp.where(z == 0, 0.0, pltpu.roll(flat, 1, 0))
    after = jnp.where(z == 15, 0.0, pltpu.roll(flat, layers * 128 - 1, 0))
    return before, flat, after


def store_shifted(out, slab, layers):
    for c, rows in enumerate(shifted_rows(slab, layers)):
        out[c, :, 1:9] = rows.astype(BF16).reshape(layers, 8, 16, C)
        out[c, :, 0] = jnp.zeros((layers, 16, C), BF16)
        out[c, :, 9] = jnp.zeros((layers, 16, C), BF16)


def patches(shifted, first, layers, back):
    rows = pl.ds(first, layers)
    return [
        (shifted[2 - c, rows, 2 - b : 10 - b] if back else shifted[c, rows, b : b + 8]).reshape(layers * 128, C)
        for b in range(3)
        for c in range(3)
    ]


def matrices(weights, k, back):
    return [weights[9 * (2 - k if back else k) + j] for j in range(9)]


def product(pieces, columns, layers, back):
    lhs = jnp.concatenate(pieces, axis=1)
    rhs = jnp.concatenate([jnp.concatenate(col, axis=1 if back else 0) for col in columns], axis=0 if back else 1)
    out = lax.dot_general(lhs, rhs, (((1,), (1 if back else 0,)), ((), ())), preferred_element_type=F32)
    out = out.reshape(layers, 128, len(columns) * C)
    return [out[:, :, n * C : (n + 1) * C] for n in range(len(columns))]


def taps(shifted, weights, layers, back=False):
    pieces = patches(shifted, 0, layers, back)
    after, same = product(pieces, [matrices(weights, 0, back), matrices(weights, 1, back)], layers, back)
    last = matrices(weights, 2, back)
    none = jnp.zeros((C, C), BF16)
    before, aside = product(pieces[:6], [last[:6], [none] * 3 + last[6:]], layers, back)
    aside = aside.reshape(layers, 8, 16, C)
    edge = jnp.zeros((layers, 1, 16, C), F32)
    moved = [edge, aside[:, :7]] if back else [aside[:, 1:], edge]
    return after, same, before + jnp.concatenate(moved, axis=1).reshape(layers, 128, C)


def inside(out, layers):
    after, same, before = out
    n = layers - 2
    return after[0:n] + same[1 : n + 1] + before[2 : n + 2]


def spread(out):
    after, same, before = out
    none = jnp.zeros((1, 128, C), F32)
    return (
        jnp.concatenate([none, none, after], axis=0)
        + jnp.concatenate([none, same, none], axis=0)
        + jnp.concatenate([before, none, none], axis=0)
    )


def completed(part, shifted, weights, back=False):
    after, left = product(
        patches(shifted, 0, 2, back), [matrices(weights, 0, back), matrices(weights, 1, back)], 2, back
    )
    right, before = product(
        patches(shifted, 2, 2, back), [matrices(weights, 1, back), matrices(weights, 2, back)], 2, back
    )
    return jnp.concatenate(
        [
            part[0:1] + after[0:1] + left[1:2],
            part[1:2] + after[1:2],
            part[2:8],
            part[8:9] + before[0:1],
            part[9:10] + right[0:1] + before[1:2],
        ],
        axis=0,
    )


def weight_terms(order, shifted_layers, padded, terms):
    turned = jnp.concatenate(
        [
            lax.dot_general(order, rows, (((1,), (1,)), ((), ())), preferred_element_type=F32).astype(BF16)
            for rows in shifted_layers
        ],
        axis=0,
    )
    rhs = jnp.concatenate([padded(a, b) for a in range(3) for b in range(3)], axis=1)
    out = jnp.dot(turned, rhs, preferred_element_type=F32)
    for a in range(3):
        for b in range(3):
            for c in range(3):
                piece = out[c * C : (c + 1) * C, (3 * a + b) * C : (3 * a + b + 1) * C]
                half, tap = divmod(9 * a + 3 * b + c, 14)
                terms[:, half, tap] = piece.astype(BF16).reshape(8, 16, C)
    terms[:, 1, 13] = jnp.zeros((8, 16, C), BF16)


def pad_store(out, slab):
    out[0:2] = jnp.zeros((2, 10, 16, C), BF16)
    out[10:12] = jnp.zeros((2, 10, 16, C), BF16)
    out[2:10, 0] = jnp.zeros((8, 16, C), BF16)
    out[2:10, 9] = jnp.zeros((8, 16, C), BF16)
    out[2:10, 1:9] = slab.astype(BF16)


def ids_of(tile):
    rows = tile.astype(F32).astype(jnp.int32)
    return [jnp.broadcast_to(rows[j : j + 1] - 1, (8, C)) for j in range(SLOTS)]


def choose(even, one, other):
    return [jnp.where(even, p, q) for p, q in zip(one, other)]


def chip_ids(own, partner, even):
    own, partner = ids_of(own[6, 0:16]), ids_of(partner[6, 0:16])
    return choose(even, own, partner), choose(even, partner, own)


def chip_kernel(
    own, partner, w_first_hbm, w_second_hbm,
    w_first, w_second, field_z, upstream_pad, act_part, grad_part,
    upstream_z, sems,
):
    thirds = [pl.ds(9 * k, 9) for k in range(3)]
    one = fetch([(w_first_hbm.at[k], w_first.at[k]) for k in thirds], sems, 0)
    even = lax.axis_index("c") == 0
    masks = [block_masks(ids) for ids in chip_ids(own, partner, even)]

    def field(which):
        partner_rows = partner[3 * which : 3 * which + 3].astype(F32).reshape(192, C)
        own_rows = own[3 * which : 3 * which + 3].astype(F32).reshape(192, C)
        parts = (
            to_slab(jnp.where(even, own_rows, partner_rows), masks[0], 4),
            to_slab(jnp.where(even, partner_rows, own_rows), masks[1], 4),
        )
        return jnp.concatenate(parts, axis=0)

    two = fetch([(w_second_hbm.at[k], w_second.at[k]) for k in thirds], sems, 3)
    store_shifted(field_z, field(0), 8)
    upstream = field(1)
    store_shifted(upstream_z, upstream, 8)
    pad_store(upstream_pad, upstream)
    for copy in one:
        copy.wait()
    for copy in two:
        copy.wait()
    act_part[...] = spread(taps(field_z, w_first, 8))
    grad_part[...] = spread(taps(upstream_z, w_second, 8, True))


def main_kernel(
    own, partner, far, near, w_first, w_second, field_z, upstream_pad, act_part, grad_part,
    terms, hidden_out, grad_out,
    outer_z, outer_up_z, stage_z, padded,
):
    core = lax.axis_index("c")
    even = core == 0
    near_ids, far_ids = ids_of(near[0, 6, 0:16]), ids_of(far[0, 6, 0:16])
    left, right = (block_masks(ids) for ids in (choose(even, near_ids, far_ids), choose(even, far_ids, near_ids)))
    lower, upper = (block_masks(ids) for ids in chip_ids(own, partner, even))

    def field(which):
        near_rows = near[0, 3 * which : 3 * which + 3].astype(F32).reshape(96, C)
        far_rows = far[0, 3 * which : 3 * which + 3].astype(F32).reshape(96, C)
        parts = (
            to_slab(jnp.where(even, near_rows, far_rows), left, 2),
            to_slab(jnp.where(even, far_rows, near_rows), right, 2),
        )
        return jnp.concatenate(parts, axis=0)

    store_shifted(outer_z, field(0), 4)
    store_shifted(outer_up_z, field(1), 4)
    first_act = completed(act_part[...], outer_z, w_first).reshape(10, 8, 16, C)
    hidden_grad = completed(grad_part[...], outer_up_z, w_second, True).reshape(10, 8, 16, C)
    live = jnp.concatenate(
        [
            live_tiles(left)[None],
            jnp.broadcast_to(live_tiles(lower)[None], (4, 8, 16, C)),
            jnp.broadcast_to(live_tiles(upper)[None], (4, 8, 16, C)),
            live_tiles(right)[None],
        ],
        axis=0,
    )
    gate = 1.0 / (1.0 + jnp.exp(-first_act))
    hidden = live * (first_act * gate)
    hidden_out[...] = hidden.astype(BF16)
    slope = live * (gate * (1.0 + first_act * (1.0 - gate)))
    grad_out[...] = (hidden_grad * slope).astype(BF16)

    @pl.when(even)
    def _():
        for c in range(3):
            stage_z[c, 0] = outer_z[c, 1, 1:9]
            stage_z[c, 1:9] = field_z[c, :, 1:9]
            stage_z[c, 9] = outer_z[c, 2, 1:9]
        pad_store(padded, grad_out[1:9])

    @pl.when(core == 1)
    def _():
        for c, rows in enumerate(shifted_rows(hidden_out[...].astype(F32), 10)):
            stage_z[c] = rows.astype(BF16).reshape(10, 8, 16, C)
        padded[...] = upstream_pad[...]

    r = lax.broadcasted_iota(jnp.int32, (C, C), 0)
    i = lax.broadcasted_iota(jnp.int32, (C, C), 1)
    y = (r // 4) % 4 * 2 + r // 64
    wanted = (((r // 2) % 2 * 8 + y) * 4 + (r // 16) % 4) * 2 + r % 2
    order = jnp.where(i == wanted, 1.0, 0.0).astype(BF16)
    weight_terms(
        order,
        [stage_z[c].reshape(1280, C) for c in range(3)],
        lambda a, b: padded[2 - a : 12 - a, 2 - b : 10 - b].reshape(1280, C),
        terms,
    )


def output_kernel(
    blocks, features, cotangent, hidden, first_grad, w_first, w_second,
    block_out, input_grad,
    hidden_z, grad_z,
):
    mine = pl.ds(4 * lax.axis_index("c"), 6)
    own = block_masks([blocks[0, j] for j in range(SLOTS)])
    store_shifted(hidden_z, hidden[mine].astype(F32), 6)
    store_shifted(grad_z, first_grad[mine].astype(F32), 6)
    second_act = from_slab(inside(taps(hidden_z, w_second, 6), 6).reshape(4, 8, 16, C), own, 4)
    back = from_slab(inside(taps(grad_z, w_first, 6, True), 6).reshape(4, 8, 16, C), own, 4)
    for j in range(SLOTS):
        live = jnp.where(blocks[0, j] < BY * BZ, 1.0, 0.0)
        block_out[0, j] = (live * (features[0, j].astype(F32) + second_act[j])).astype(BF16)
        input_grad[0, j] = (live * (cotangent[0, j].astype(F32) + back[j])).astype(BF16)


def repeat_kernel(pieces, out):
    total = pieces[0]
    for k in range(1, 4):
        total = total + pieces[k]
    total = total.astype(BF16)
    for n in range(4):
        for k in range(6):
            out[6 * n + k] = total[n]


def last_kernel(pieces, first, second):
    for c, out in enumerate((first, second)):
        for sb, rows in enumerate((14, 13)):
            parts = [pieces[zh * 12 + c * 6 + sa * 2 + sb].astype(F32) for zh in range(2) for sa in range(3)]
            total = parts[0]
            for part in parts[1:]:
                total = total + part
            out[14 * sb : 14 * sb + rows] = total[0:rows]


VMEM = pl.BlockSpec(memory_space=pltpu.VMEM)
SMEM = pl.BlockSpec(memory_space=pltpu.SMEM)
HBM = pl.BlockSpec(memory_space=pltpu.HBM)


def kernel_call(body, ins, outs, scratch, flops, room=50):
    return pl.pallas_call(
        body,
        out_shape=outs,
        in_specs=ins,
        out_specs=[VMEM] * len(outs),
        scratch_shapes=scratch,
        compiler_params=pltpu.CompilerParams(vmem_limit_bytes=room * 1024 * 1024),
        cost_estimate=pl.CostEstimate(flops=flops, bytes_accessed=4_000_000, transcendentals=0),
    )


def in_hbm(*arrays):
    return [pltpu.with_memory_space_constraint(a, pltpu.HBM) for a in arrays]


def shape(*dims, dtype=BF16):
    return jax.ShapeDtypeStruct(dims, dtype)


def folded(pieces):
    return pieces.astype(F32).sum(axis=0)


def on_device(features, cotangent, blocks, w_first, w_second):
    outer, inner = kernel_call(
        halo_kernel,
        [HBM] * 3,
        [shape(1, 7, 32, C), shape(7, 64, C)],
        [pltpu.SMEM((1, SLOTS), jnp.int32), pltpu.SemaphoreType.DMA((5,))],
        1,
        40,
    )(*in_hbm(blocks, features, cotangent))
    odd = range(1, 127, 2)
    partner = lax.ppermute(inner, "c", [(0, 1), (1, 0)])
    far = lax.ppermute(outer, TILE, [(t + 2, t) for t in range(0, 126, 2)] + [(t, t + 2) for t in range(1, 126, 2)])
    near = lax.ppermute(outer, TILE, [(t, t + 1) for t in odd] + [(t + 1, t) for t in odd])
    w_first, w_second, field_z, upstream_pad, act_part, grad_part = kernel_call(
        chip_kernel,
        [VMEM, VMEM, HBM, HBM],
        [
            shape(27, C, C),
            shape(27, C, C),
            shape(3, 8, 10, 16, C),
            shape(12, 10, 16, C),
            shape(10, 128, C, dtype=F32),
            shape(10, 128, C, dtype=F32),
        ],
        [pltpu.VMEM((3, 8, 10, 16, C), BF16), pltpu.SemaphoreType.DMA((6,))],
        2_000_000_000,
        40,
    )(inner, partner, *in_hbm(w_first, w_second))
    terms, hidden, first_grad = kernel_call(
        main_kernel,
        [VMEM] * 10,
        [shape(8, 2, 14, 16, C), shape(10, 8, 16, C), shape(10, 8, 16, C)],
        [
            pltpu.VMEM((3, 4, 10, 16, C), BF16),
            pltpu.VMEM((3, 4, 10, 16, C), BF16),
            pltpu.VMEM((3, 10, 8, 16, C), BF16),
            pltpu.VMEM((12, 10, 16, C), BF16),
        ],
        2_000_000_000,
        40,
    )(inner, partner, far, near, w_first, w_second, field_z, upstream_pad, act_part, grad_part)
    block_out, input_grad = kernel_call(
        output_kernel,
        [SMEM] + [VMEM] * 6,
        [shape(1, SLOTS, 64, C)] * 2,
        [pltpu.VMEM((3, 6, 10, 16, C), BF16), pltpu.VMEM((3, 6, 10, 16, C), BF16)],
        1_400_000_000,
    )(blocks, features, cotangent, hidden, first_grad, w_first, w_second)
    terms = terms.reshape(16, 14, 16, C)
    along_x = folded(lax.all_to_all(terms, ("yb", "x", "sb"), 0, 0, tiled=True)).reshape(14, 4, 4, C)
    along_y = lax.all_to_all(along_x.transpose(1, 2, 0, 3), "ya", 0, 0, tiled=True)
    copies = kernel_call(repeat_kernel, [VMEM], [shape(24, 14, C)], [], 1, 40)(along_y)[0]
    pieces = lax.all_to_all(copies, ("zh", "c", "sa", "sb"), 0, 0, tiled=True)
    first_total, second_total = kernel_call(last_kernel, [VMEM], [shape(27, C, dtype=F32)] * 2, [], 1, 40)(pieces)
    return block_out, input_grad, first_total, second_total


def solution(mesh):
    split = Mesh(mesh.devices.reshape(2, 4, 2, 4, 2, 3, 2), TILE + SCENE)
    return jax.shard_map(
        on_device,
        mesh=split,
        in_specs=(
            P(SCENE, TILE, None, None),
            P(SCENE, TILE, None, None),
            P(SCENE, TILE),
            P(),
            P(),
        ),
        out_specs=(
            P(SCENE, TILE, None, None),
            P(SCENE, TILE, None, None),
            P(None, TILE),
            P(None, TILE),
        ),
        check_vma=False,
    )
```
